128 devices in a mesh: seq: 4 (over x), vocab: 32 (over y, z, core).
Axes of the slice: x: 4, y: 4, z: 4, core: 2. Of those that a mesh axis runs over, the one named last changes fastest.
Arguments:
- teacher_hidden: bfloat16 [768, 8192], P('seq'), may hold values from -125 to 125, as said below
- teacher_weight: bfloat16 [8192, 65536], P('seq', 'vocab'), may hold values from -0.0625 to 0.0625
- student_hidden: bfloat16 [768, 3072], P(('seq', 'vocab')), may hold values from -125 to 125, as said below
- student_weight: bfloat16 [3072, 32, 2048], P(None, 'vocab', 'seq'), may hold values from -0.109375 to 0.109375
Outputs:
- loss: float32 [], replicated
- grad_hidden: bfloat16 [768, 3072], P(('seq', 'vocab'))
- grad_weight: float32 [3072, 32, 2048], P(None, 'vocab', 'seq')
The draws below stay inside these ranges and needn't reach their ends.
Inputs may be any that keep to these rules, and one draw needn't show every extreme that they name: `teacher_hidden`: teacher hidden entries lie within this range. `student_hidden`: student hidden entries lie within this range.
All inputs are finite; a program needn't handle non-finite values.
Results may differ from the reference program's by a relative error of at most 0.0085.
Values may be sent and summed in bfloat16 or wider, within the bound.
No kernel may reach another device: no remote copies, remote signals or barrier semaphores. Data moves between devices by JAX's collectives and lax.ppermute only.
A program may use at most 128 MiB of HBM per device.

```python
import jax
import jax.numpy as jnp
from jax import lax

D_T = 8192
D_S = 3072
VOCAB = 65536
TOKENS = 768
TEACHER_COLS = 2048
N_VOCAB = 32


def drawn_rows(key, rows, cols):
    return jnp.clip(3.0 * jax.random.normal(key, (rows, cols), jnp.float32), -15.0, 15.0)


def draw_teacher_hidden(key, part):
    key = jax.random.fold_in(key, 11)
    return drawn_rows(key, TOKENS, D_T).astype(jnp.bfloat16)


def draw_student_hidden(key, part):
    key = jax.random.fold_in(key, 23)
    return drawn_rows(key, TOKENS, D_S).astype(jnp.bfloat16)


def level_of(stream_key, dims, shards, least, top_value):
    loudness, own = 1.0, jax.random.fold_in(stream_key, 6)
    for position, parts in shards:
        draws = jnp.exp(jax.random.uniform(jax.random.fold_in(own, position), (parts,), jnp.float32, least / len(shards), top_value / len(shards)))
        loudness = loudness * jnp.repeat(draws, dims[position] // parts).reshape([-1 if axis == position else 1 for axis in range(len(dims))])
    return loudness


def gaussian(rng, dims, width, bound, pieces=(), kind=jnp.bfloat16):
    array = jax.random.normal(rng, dims, jnp.float32) * width
    if len(pieces) > 0:
        array = level_of(rng, dims, pieces, -0.22, 0.18) * array
    return jnp.clip(array, min=-bound, max=bound).astype(kind)


def setup_inputs(seed: int = 0) -> dict:
    key_list = jax.random.split(jax.random.key(seed), 5)
    teacher_hidden = draw_teacher_hidden(jax.random.fold_in(key_list[4], 71), 0)
    teacher_weight = gaussian(key_list[1], (D_T, VOCAB), D_T ** -0.5, 0.0625, ((0, 4), (1, 32)))
    student_hidden = draw_student_hidden(jax.random.fold_in(key_list[4], 71), 0)
    student_weight = gaussian(key_list[3], (D_S, N_VOCAB, TEACHER_COLS), D_S ** -0.5, 0.109375, ((1, 32), (2, 4)))
    return {"teacher_hidden": teacher_hidden, "teacher_weight": teacher_weight, "student_hidden": student_hidden, "student_weight": student_weight}


grad_scale = 64.0


def reference(teacher_hidden, teacher_weight, student_hidden, student_weight):
    teacher_logits = jnp.dot(teacher_hidden, teacher_weight, preferred_element_type=jnp.float32)
    weight_flat = student_weight.reshape(D_S, VOCAB)
    student_logits = jnp.dot(student_hidden, weight_flat, preferred_element_type=jnp.float32)
    t_max = jnp.max(teacher_logits, axis=1)
    s_max = jnp.max(student_logits, axis=1)
    t_exp = jnp.exp(teacher_logits - t_max[:, None])
    s_exp = jnp.exp(student_logits - s_max[:, None])
    t_sum = jnp.sum(t_exp, axis=1)
    s_sum = jnp.sum(s_exp, axis=1)
    cross = jnp.sum(t_exp * (teacher_logits - student_logits), axis=1)
    kl_rows = cross / t_sum - t_max - jnp.log(t_sum) + s_max + jnp.log(s_sum)
    loss = jnp.mean(kl_rows)
    grad_logits = (grad_scale * (s_exp / s_sum[:, None] - t_exp / t_sum[:, None])).astype(jnp.bfloat16)
    grad_hidden = lax.dot_general(grad_logits, weight_flat, (((1,), (1,)), ((), ())), preferred_element_type=jnp.float32).astype(jnp.bfloat16)
    grad_flat = lax.dot_general(student_hidden, grad_logits, (((0,), (0,)), ((), ())), preferred_element_type=jnp.float32)
    return loss, grad_hidden, grad_flat.reshape(D_S, N_VOCAB, TEACHER_COLS)
```

```python
import jax
import jax.numpy as jnp
import numpy as np
from jax import lax
from jax.sharding import Mesh
from jax.sharding import PartitionSpec as P

grad_scale = 64.0
GROUPS = 2
ALL = ("x", "y", "z", "c")
CHIPS = ("x", "y", "z")
SWAP = [(0, 1), (1, 0)]


def shift(k, n):
    return [(i, (i + k) % n) for i in range(n)]


def row_order(rows, groups):
    piece = rows // 32
    order = np.arange(rows).reshape(16, groups, 32 // groups // 16 * piece).transpose(1, 0, 2).reshape(-1)
    return np.eye(rows, dtype=np.float32)[order]


def merge(parts):
    t_max = jnp.max(parts[:, 0], axis=0)
    s_max = jnp.max(parts[:, 3], axis=0)
    t_w = jnp.exp(parts[:, 0] - t_max)
    s_w = jnp.exp(parts[:, 3] - s_max)
    return jnp.stack(
        [t_max, jnp.sum(parts[:, 1] * t_w, 0), jnp.sum(parts[:, 2] * t_w, 0), s_max, jnp.sum(parts[:, 4] * s_w, 0)]
    )


def shards(th, tw, sh, sw):
    x, c = lax.axis_index("x"), lax.axis_index("c")
    rows, d_t = th.shape
    ks, cols = tw.shape
    d_s, _, own = sw.shape
    n_x = d_t // ks
    tokens = rows * n_x
    n = rows // GROUPS
    nh = n // 2
    w = sw[:, 0, :]
    if GROUPS > 1:
        th = jnp.dot(jnp.asarray(row_order(rows, GROUPS), jnp.bfloat16), th, preferred_element_type=jnp.float32).astype(jnp.bfloat16)

    gathered = lax.all_gather(sh, ALL, axis=0, tiled=False)
    piece = sh.shape[0]
    hs = gathered.reshape(64, GROUPS, 2 // GROUPS * piece, d_s).transpose(1, 0, 2, 3).reshape(GROUPS, tokens // GROUPS, d_s)

    hidden = []
    after = None
    for g in range(GROUPS):
        sends = [
            lax.dynamic_slice(th, (g * n + c * nh, ((x + k) % n_x) * ks), (nh, ks)) for k in range(1, n_x)
        ]
        if after is not None:
            sends, _ = lax.optimization_barrier((sends, after))
        got = [lax.ppermute(s, "x", shift(k + 1, n_x)) for k, s in enumerate(sends)]
        other = [lax.ppermute(s, "c", SWAP) for s in got]
        after = got
        buf = jnp.zeros((n_x, n, ks), th.dtype)
        buf = lax.dynamic_update_slice(buf, lax.dynamic_slice(th, (g * n, x * ks), (n, ks))[None], (x, 0, 0))
        for k in range(1, n_x):
            src = (x - k + n_x) % n_x
            buf = lax.dynamic_update_slice(buf, got[k - 1][None], (src, c * nh, 0))
            buf = lax.dynamic_update_slice(buf, other[k - 1][None], (src, (1 - c) * nh, 0))
        hidden.append(buf.reshape(n_x * n, ks))

    def part(h, j):
        block = lax.dynamic_slice(tw, (0, ((x + j) % n_x) * own), (ks, own))
        return jnp.dot(h, block, preferred_element_type=jnp.float32)

    half = n_x * n // 2
    teacher = []
    after = None
    for g in range(GROUPS):
        hr, hl = hidden[g][:half], hidden[g][half:]
        if after is not None:
            (hr, hl), _ = lax.optimization_barrier(((hr, hl), after))
        right = left = None
        for t in range(n_x - 1):
            r = part(hr, n_x - 1 - t)
            l = part(hl, 1 + t)
            if t:
                r, l = r + right, l + left
            if t == n_x - 2:
                after = (r, l)
            right = lax.ppermute(r, "x", shift(1, n_x))
            left = lax.ppermute(l, "x", shift(-1, n_x))
        teacher.append(jnp.concatenate([part(hr, 0) + right, part(hl, 0) + left], axis=0))

    loss = 0.0
    grads = []
    halves = []
    for g in range(GROUPS):
        tl = teacher[g]
        sl = jnp.dot(hs[g], w, preferred_element_type=jnp.float32)
        t_loc, s_loc = jnp.max(tl, axis=1), jnp.max(sl, axis=1)
        te = jnp.exp(tl - t_loc[:, None])
        se = jnp.exp(sl - s_loc[:, None])
        st = jnp.stack([t_loc, jnp.sum(te, 1), jnp.sum(te * (tl - sl), 1), s_loc, jnp.sum(se, 1)])
        st = merge(jnp.stack([st, lax.ppermute(st, "c", SWAP)]))
        sent = jnp.broadcast_to(st[None], (64,) + st.shape)
        st = merge(lax.all_to_all(sent, CHIPS, split_axis=0, concat_axis=0, tiled=True))
        t_max, t_sum, cross, s_max, s_sum = st
        loss = loss + jnp.sum(cross / t_sum - t_max - jnp.log(t_sum) + s_max + jnp.log(s_sum))
        grad = (
            grad_scale
            * (
                jnp.exp(sl - s_max[:, None]) / s_sum[:, None]
                - jnp.exp(tl - t_max[:, None]) / t_sum[:, None]
            )
        ).astype(jnp.bfloat16)
        grads.append(grad)
        per = n_x * n // 64
        room = -(-per // 8) * 8
        padded = jnp.pad(grad.reshape(64, per, own), ((0, 0), (0, room - per), (0, 0))).reshape(64 * room, own)
        dims = (((1,), (1,)), ((), ()))
        away = lax.dynamic_slice(w, ((1 - c) * (d_s // 2), 0), (d_s // 2, own))
        keep = lax.dynamic_slice(w, (c * (d_s // 2), 0), (d_s // 2, own))
        away = lax.dot_general(padded, away, dims, preferred_element_type=jnp.float32).astype(jnp.bfloat16)
        keep = lax.dot_general(padded, keep, dims, preferred_element_type=jnp.float32)
        chip = (keep + lax.ppermute(away, "c", SWAP).astype(jnp.float32)).astype(jnp.bfloat16)
        chip = lax.all_to_all(chip.reshape(64, room, d_s // 2), CHIPS, split_axis=0, concat_axis=0, tiled=True)
        halves.append(jnp.sum(chip.astype(jnp.float32), axis=0)[:per])
    loss = loss / tokens

    both = jnp.concatenate(halves, axis=0).reshape(2, piece, d_s // 2)
    mine = lax.dynamic_index_in_dim(both, c, 0, keepdims=False).astype(jnp.bfloat16)
    theirs = lax.dynamic_index_in_dim(both, 1 - c, 0, keepdims=False).astype(jnp.bfloat16)
    got = lax.ppermute(theirs, "c", SWAP)
    grad_hidden = jnp.where(c == 0, jnp.concatenate([mine, got], 1), jnp.concatenate([got, mine], 1))
    grad_weight = lax.dot_general(
        hs.reshape(tokens, d_s), jnp.concatenate(grads, 0), (((0,), (0,)), ((), ())), preferred_element_type=jnp.float32
    )
    return (loss, grad_hidden, grad_weight[:, None, :])


def solution(mesh):
    mesh = Mesh(mesh.devices.reshape(4, 4, 4, 2), ALL)
    vocab = ("y", "z", "c")
    in_specs = (P("x", None), P("x", vocab), P(ALL, None), P(None, vocab, "x"))
    out_specs = (P(), P(ALL, None), P(None, vocab, "x"))
    return jax.shard_map(shards, mesh=mesh, in_specs=in_specs, out_specs=out_specs, check_vma=False)
```

```python
import functools

import jax
import jax.numpy as jnp
import numpy as np
from jax import lax
from jax.experimental import pallas as pl
from jax.experimental.pallas import tpu as pltpu
from jax.sharding import Mesh
from jax.sharding import PartitionSpec as P

grad_scale = 64.0
ROWS = (8, 4)
ALL = ("x", "y", "z", "c")
CHIPS = ("x", "y", "z")
SWAP = [(0, 1), (1, 0)]
F32, BF16 = jnp.float32, jnp.bfloat16
NT = (((1,), (1,)), ((), ()))
TN = (((0,), (0,)), ((), ()))
VMEM_BYTES = 20 * 2**20


def shift(k):
    return [(i, (i + k) % 4) for i in range(4)]


def dot(a, b, dims=(((1,), (0,)), ((), ()))):
    return lax.dot_general(a, b, dims, preferred_element_type=F32)


def call(body, scalars, args, in_specs, outs, out_specs, grid=(1,), scratch=(), flops=0):
    nbytes = sum(a.size * a.dtype.itemsize for a in list(args) + list(outs))
    return pl.pallas_call(
        body,
        out_shape=outs,
        grid_spec=pltpu.PrefetchScalarGridSpec(
            num_scalar_prefetch=1, grid=grid, in_specs=in_specs, out_specs=out_specs, scratch_shapes=scratch
        ),
        compiler_params=pltpu.CompilerParams(vmem_limit_bytes=VMEM_BYTES),
        cost_estimate=pl.CostEstimate(flops=flops, bytes_accessed=nbytes, transcendentals=0),
    )(scalars, *args)


def whole(shape):
    return pl.BlockSpec(shape, lambda *_: (0,) * len(shape))


def sds(shape, dtype):
    return jax.ShapeDtypeStruct(shape, dtype)


def cut_body(where, order, th, own, *sends):
    ks = th.shape[1] // 4
    x, c = where[0], where[1]
    halves = []
    for s, n in ((0, 16 * ROWS[0]), (16 * ROWS[0], 16 * ROWS[1])):
        halves.append(order[pl.ds(pl.multiple_of(s + c * (n // 2), n // 2), n // 2), :])
    pick = jnp.concatenate(halves, axis=0)
    for k in (1, 2, 3):
        block = th[:, pl.ds(pl.multiple_of(lax.rem(x + k, 4) * ks, ks), ks)]
        sends[k - 1][...] = dot(pick, block).astype(BF16)
    block = th[:, pl.ds(pl.multiple_of(x * ks, ks), ks)]
    own[...] = dot(order[...], block).astype(BF16)


def cut(where, order, th):
    rows, d = th.shape
    ks = d // 4
    outs = [sds((rows, ks), BF16)] + [sds((rows // 2, ks), BF16)] * 3
    return call(
        cut_body, where, (order, th), [whole(order.shape), whole(th.shape)], outs, [whole(o.shape) for o in outs],
        flops=4 * rows * rows * d,
    )


def first_body(group, where, own, g1, g2, g3, o1, o2, o3, tw, h, r, l, wr, wl, sems):
    n = 16 * ROWS[group]
    nh = n // 2
    at = 16 * ROWS[0] * group
    x, c = where[0], where[1]
    cols = wr.shape[1]
    copies = []
    for i, (step, to) in enumerate(((3, wr), (1, wl))):
        block = tw.at[:, pl.ds(pl.multiple_of(lax.rem(x + step, 4) * cols, cols), cols)]
        copies.append(pltpu.make_async_copy(block, to, sems.at[i]))
        copies[-1].start()
    h[pl.ds(pl.multiple_of(x * n, n), n), :] = own[at : at + n, :]
    at = at // 2
    for k, (a, b) in enumerate(((g1, o1), (g2, o2), (g3, o3))):
        to = lax.rem(x + 3 - k, 4) * n
        h[pl.ds(pl.multiple_of(to + c * nh, nh), nh), :] = a[at : at + nh, :]
        h[pl.ds(pl.multiple_of(to + (1 - c) * nh, nh), nh), :] = b[at : at + nh, :]
    copies[0].wait()
    r[...] = dot(h[: 2 * n, :], wr[...])
    copies[1].wait()
    l[...] = dot(h[2 * n :, :], wl[...])


def first(where, group, own, got, other, tw):
    n, ks = 16 * ROWS[group], own.shape[1]
    cols = tw.shape[1] // 4
    outs = [sds((4 * n, ks), BF16), sds((2 * n, cols), F32), sds((2 * n, cols), F32)]
    pieces = [own, *got, *other]
    specs = [whole(p.shape) for p in pieces] + [pl.BlockSpec(memory_space=pltpu.HBM)]
    body = functools.partial(first_body, group)
    scratch = [pltpu.VMEM((ks, cols), BF16)] * 2 + [pltpu.SemaphoreType.DMA((2,))]
    return call(
        body, where, (*pieces, tw), specs, outs, [whole(o.shape) for o in outs], scratch=scratch, flops=8 * n * ks * cols
    )


def rest_body(where, h, w, wl, out):
    half = h.shape[0] // 2
    step = pl.program_id(0)

    @pl.when(step != 1)
    def _():
        out[0] = dot(h[...], w[...])

    @pl.when(step == 1)
    def _():
        out[0, :half, :] = dot(h[:half, :], w[...])
        out[0, half:, :] = dot(h[half:, :], wl[...])


def rest(where, h, tw):
    rows, ks = h.shape
    cols = tw.shape[1] // 4
    out = sds((3, rows, cols), F32)
    specs = [
        whole(h.shape),
        pl.BlockSpec((ks, cols), lambda i, w: (0, lax.rem(w[0] + 6 - i, 4))),
        pl.BlockSpec((ks, cols), lambda i, w: (0, lax.rem(w[0] + 3, 4))),
    ]
    step = pl.BlockSpec((1, rows, cols), lambda i, w: (i, 0, 0))
    return call(rest_body, where, (h, tw, tw), specs, [out], [step], grid=(3,), flops=6 * rows * ks * cols)[0]


def hop_body(where, p, right, left, r, l):
    half = right.shape[0]
    r[...] = p[0, :half, :] + right[...]
    l[...] = p[0, half:, :] + left[...]


def hop(where, p, step, right, left):
    half, cols = right.shape
    out = sds(right.shape, F32)
    specs = [pl.BlockSpec((1, 2 * half, cols), lambda i, w: (step, 0, 0)), whole(right.shape), whole(left.shape)]
    return call(hop_body, where, (p, right, left), specs, [out, out], [whole(out.shape)] * 2)


def student_body(where, pick_mine, pick_other, mine, other, w, hs, sl):
    rows = (dot(pick_mine[...], mine[...]) + dot(pick_other[...], other[...])).astype(BF16)
    hs[...] = rows

    @pl.when(pl.program_id(0) == 0)
    def _():
        sl[...] = jnp.zeros_like(sl)

    sl[...] += dot(rows, w[...])


def student(where, picks, mine, other, w):
    tokens, room = picks[0].shape
    d, cols = w.shape
    tile = d // 6
    block = pl.BlockSpec((room, tile), lambda i, s: (0, i))
    specs = [whole((tokens, room))] * 2 + [block, block, pl.BlockSpec((tile, cols), lambda i, s: (i, 0))]
    outs = [sds((tokens, d), BF16), sds((tokens, cols), F32)]
    return call(
        student_body, where, (*picks, mine, other, w), specs, outs,
        [pl.BlockSpec((tokens, tile), lambda i, s: (0, i)), whole(outs[1].shape)],
        grid=(6,), flops=2 * tokens * d * (2 * room + cols),
    )


def local_body(where, p, rr, lr, sl, *rest):
    tl, st = rest[-2:]
    half, cols = rr.shape
    tl[:half, :] = p[0, :half, :] + rr[...]
    tl[half:, :] = p[0, half:, :] + lr[...]
    t, s = tl[...], sl[...]
    t_max = jnp.max(t, axis=1, keepdims=True)
    s_max = jnp.max(s, axis=1, keepdims=True)
    te = jnp.exp(t - t_max)
    t_sum = jnp.sum(te, axis=1, keepdims=True)
    cross = jnp.sum(te * (t - s), axis=1, keepdims=True)
    s_sum = jnp.sum(jnp.exp(s - s_max), axis=1, keepdims=True)
    lane = lax.broadcasted_iota(jnp.int32, (2 * half, 128), 1)
    packed = jnp.zeros((2 * half, 128), F32)
    for i, v in enumerate((t_max, t_sum, cross, s_max, s_sum)):
        packed = jnp.where(lane == i, v, packed)
    if len(rest) == 3:
        st[:, : rest[0].shape[1]] = rest[0][...]
    st[:, st.shape[1] - 2 * half :] = jnp.transpose(packed)[:8, :]


def local(where, p, right, left, sl, at, earlier=None):
    half, cols = right.shape
    n = 2 * half
    args = (p, right, left, sl) + (() if earlier is None else (earlier,))
    outs = [sds((n, cols), F32), sds((8, n if earlier is None else n + earlier.shape[1]), F32)]
    specs = [
        pl.BlockSpec((1, n, cols), lambda i, s: (2, 0, 0)),
        whole(right.shape),
        whole(left.shape),
        pl.BlockSpec((n, cols), lambda i, s: (at, 0)),
    ] + [whole(a.shape) for a in args[4:]]
    return call(local_body, where, args, specs, outs, [whole(o.shape) for o in outs], flops=40 * half * cols)


def merged(parts):
    t_max = jnp.max(parts[0], axis=0, keepdims=True)
    s_max = jnp.max(parts[3], axis=0, keepdims=True)
    t_w = jnp.exp(parts[0] - t_max)
    s_w = jnp.exp(parts[3] - s_max)
    total = lambda v: jnp.sum(v, axis=0, keepdims=True)
    return [t_max, total(parts[1] * t_w), total(parts[2] * t_w), s_max, total(parts[4] * s_w)]


def spread_body(where, mine, other, out):
    lead = where[1] == 0
    a = jnp.where(lead, mine[...], other[...])
    b = jnp.where(lead, other[...], mine[...])
    t_max, s_max = jnp.maximum(a[0:1], b[0:1]), jnp.maximum(a[3:4], b[3:4])
    ta, tb = jnp.exp(a[0:1] - t_max), jnp.exp(b[0:1] - t_max)
    sa, sb = jnp.exp(a[3:4] - s_max), jnp.exp(b[3:4] - s_max)
    rows = [t_max, a[1:2] * ta + b[1:2] * tb, a[2:3] * ta + b[2:3] * tb, s_max, a[4:5] * sa + b[4:5] * sb]
    chip = jnp.concatenate(rows + [jnp.zeros_like(a[:3])], axis=0)
    out[...] = jnp.broadcast_to(chip[None], out.shape)


def spread(where, mine, other):
    out = sds((64,) + mine.shape, F32)
    return call(spread_body, where, (mine, other), [whole(mine.shape)] * 2, [out], [whole(out.shape)])[0]


def back(grad, place, w):
    if place is None:
        return dot(grad, w[...], NT)
    half = w.shape[0] // 2
    top = dot(dot(place[0], grad).astype(BF16), w[:half, :], NT)
    return top + dot(dot(place[1], grad).astype(BF16), w[half:, :], NT)


def grad_body(where, parts, tl, sl, w, *rest):
    place = rest[0] if len(rest) == 4 else None
    g, away, kl = rest[-3:]
    t_max, t_sum, cross, s_max, s_sum = merged([parts[:, i, :] for i in range(5)])
    rows = cross / t_sum - t_max - jnp.log(t_sum) + s_max + jnp.log(s_sum)
    kl[...] = jnp.broadcast_to(jnp.sum(rows, axis=1, keepdims=True), kl.shape)
    stats = jnp.concatenate([t_max, grad_scale / t_sum, s_max, grad_scale / s_sum], axis=0)
    stats = jnp.concatenate([stats, jnp.zeros((124, stats.shape[1]), F32)], axis=0)
    cols = jnp.transpose(stats)
    grad = jnp.exp(sl[...] - cols[:, 2:3]) * cols[:, 3:4] - jnp.exp(tl[...] - cols[:, 0:1]) * cols[:, 1:2]
    grad = grad.astype(BF16)
    g[...] = grad
    away[...] = back(grad, place, w).astype(BF16)


def back_shape(tokens, d, place):
    return (tokens, d // 2) if place is None else (place.shape[1], d // 4)


def grad_of(where, parts, tl, sl, at, w, place):
    tokens, cols = tl.shape
    d = w.shape[0]
    outs = [sds((tokens, cols), BF16), sds(back_shape(tokens, d, place), BF16), sds((8, 128), F32)]
    args = (parts, tl, sl, w) + (() if place is None else (place,))
    specs = [whole(a.shape) for a in args]
    specs[0] = pl.BlockSpec((64, 8, tokens), lambda i, s: (0, 0, at))
    specs[2] = pl.BlockSpec((tokens, cols), lambda i, s: (at, 0))
    specs[3] = pl.BlockSpec((d // 2, cols), lambda i, s: (1 - s[1], 0))
    return call(grad_body, where, args, specs, outs, [whole(o.shape) for o in outs], flops=tokens * cols * d)


def keep_body(where, g, w, *rest):
    rest[-1][...] = back(g[...], rest[0] if len(rest) == 2 else None, w)


def keep_of(where, g, w, place):
    tokens, cols = g.shape
    d = w.shape[0]
    out = sds(back_shape(tokens, d, place), F32)
    args = (g, w) + (() if place is None else (place,))
    specs = [whole(a.shape) for a in args]
    specs[1] = pl.BlockSpec((d // 2, cols), lambda i, s: (s[1], 0))
    return call(keep_body, where, args, specs, [out], [whole(out.shape)], flops=tokens * cols * d)[0]


def weight_body(where, hs, ga, gb, out, done):
    n = ga.shape[0]
    out[...] = (dot(hs[:n, :], ga[...], TN) + dot(hs[n:, :], gb[...], TN))[:, None, :]
    done[...] = jnp.zeros_like(done)


def weight_of(where, hs, gs):
    tokens, d = hs.shape
    cols = gs[0].shape[1]
    tile = 256
    outs = [sds((d, 1, cols), F32), sds((8, 128), F32)]
    specs = [pl.BlockSpec((tokens, tile), lambda i, s: (0, i))] + [whole(g.shape) for g in gs]
    return call(
        weight_body, where, (hs, *gs), specs, outs,
        [pl.BlockSpec((tile, 1, cols), lambda i, s: (i, 0, 0)), whole((8, 128))],
        grid=(d // tile,), flops=2 * tokens * d * cols,
    )


def row_order(rows):
    chips = np.arange(rows).reshape(16, -1)
    order = np.concatenate([chips[:, : ROWS[0]].reshape(-1), chips[:, ROWS[0] :].reshape(-1)])
    return np.eye(rows, dtype=np.float32)[order]


def place_of(m):
    if m == 8:
        return None
    place = np.zeros((2, 64, 2, m, 64, m), np.float32)
    for chip in range(64):
        for r in range(m):
            for h in range(2):
                place[h, chip, h, r, chip, r] = 1.0
    return jnp.asarray(place.reshape(2, 128 * m, 64 * m), BF16)


def picks_of(x, c, start, m, piece):
    i = jnp.arange(64 * m)
    row = start + i % m
    at = i % (16 * m) // m * 32 + (x + 4 - i // (16 * m)) % 4 * 8 + row % piece
    hit = at[:, None] == jnp.arange(512)[None, :]
    own = (row // piece == c)[:, None]
    return (hit & own).astype(BF16), (hit & ~own).astype(BF16)


def tie(values, *after):
    return lax.optimization_barrier((values, after))[0]


def shards(th, tw, sh, sw):
    x, c = lax.axis_index("x"), lax.axis_index("c")
    where = jnp.stack([x, c]).astype(jnp.int32)
    rows = th.shape[0]
    piece, d_s = sh.shape
    w = sw[:, 0, :]
    picks = [picks_of(x, c, s, m, piece) for s, m in zip((0, ROWS[0]), ROWS)]
    picks = [jnp.concatenate(p, axis=0) for p in zip(*picks)]
    places = [place_of(m) for m in ROWS]
    at = (0, 4 * 16 * ROWS[0] // (4 * 16 * ROWS[1]))

    def exchange(sends):
        return [lax.ppermute(s, "x", shift(k + 1)) for k, s in enumerate(sends)]

    def both_ways(r, l):
        return lax.ppermute(r, "x", shift(1)), lax.ppermute(l, "x", shift(-1))

    def swap(v):
        return lax.ppermute(v, "c", SWAP)

    own, *sends = cut(where, jnp.asarray(row_order(rows), BF16), th)
    got = [lax.ppermute(s, "x", shift(k + 1)) for k, s in enumerate(sends)]

    sh8 = jnp.pad(tie(sh, own), ((0, 8 - piece), (0, 0)))
    row = jnp.concatenate([sh8] + [lax.ppermute(sh8, "x", shift(k)) for k in (1, 2, 3)], axis=0)
    mine = lax.all_gather(row, ("y", "z"), axis=0, tiled=True)

    other = [swap(v) for v in got]
    h_a, r0_a, l0_a = first(where, 0, own, got, other, tw)
    right_a, left_a = both_ways(r0_a, l0_a)
    h_b, r0_b, l0_b = first(where, 1, tie(own, r0_a), got, other, tw)
    right_b, left_b = both_ways(r0_b, l0_b)
    p_a = rest(where, tie(h_a, r0_b), tw)
    r1_a, l1_a = hop(where, p_a, 0, right_a, left_a)
    right_a, left_a = both_ways(r1_a, l1_a)
    p_b = rest(where, tie(h_b, r1_a), tw)
    r1_b, l1_b = hop(where, p_b, 0, right_b, left_b)
    right_b, left_b = both_ways(r1_b, l1_b)
    r2_a, l2_a = hop(where, p_a, 1, right_a, tie(left_a, r1_b))
    right_a, left_a = both_ways(r2_a, l2_a)
    r2_b, l2_b = hop(where, p_b, 1, right_b, tie(left_b, r2_a))
    right_b, left_b = both_ways(r2_b, l2_b)
    mine = tie(mine, r2_b)
    theirs = swap(mine)
    hs, sl = student(where, picks, mine, theirs, w)
    tl_a, st_a = local(where, p_a, right_a, left_a, sl, at[0])
    tl_b, st = local(where, p_b, right_b, left_b, sl, at[1], st_a)
    sent = spread(where, st, swap(st))
    parts = lax.all_to_all(sent, CHIPS, split_axis=0, concat_axis=0, tiled=True)

    def finish(parts, tl, g):
        grad, away, kl = grad_of(where, parts, tl, sl, at[g], w, places[g])
        got = swap(away)
        chip = (keep_of(where, grad, w, places[g]) + got.astype(F32)).astype(BF16)
        return grad, chip.reshape(64, 8, -1), kl[0, 0]

    def scatter(chip):
        return lax.all_to_all(chip, CHIPS, split_axis=0, concat_axis=0, tiled=True)

    def total(parts):
        return jnp.sum(parts.astype(F32), axis=0).astype(BF16)

    g_a, chip_a, kl_a = finish(parts, tl_a, 0)
    to_a = scatter(chip_a)
    g_b, chip_b, kl_b = finish(tie(parts, chip_a), tl_b, 1)
    to_b = scatter(chip_b)
    loss = (kl_a + kl_b) / (4 * rows)
    grad_weight, done = weight_of(where, hs, tie((g_a, g_b), chip_b))

    sum_a = total(tie(to_a, done))
    sum_b = total(tie(to_b, done)).reshape(2, ROWS[1], -1).transpose(1, 0, 2).reshape(ROWS[1], -1)
    both = jnp.concatenate([sum_a, sum_b], axis=0)
    cores = (both[:piece], both[piece:])
    mine = jnp.where(c == 0, *cores)
    got = swap(jnp.where(c == 0, cores[1], cores[0]))
    grad_hidden = jnp.where(c == 0, jnp.concatenate([mine, got], 1), jnp.concatenate([got, mine], 1))
    return (loss, grad_hidden, grad_weight)


def solution(mesh):
    mesh = Mesh(mesh.devices.reshape(4, 4, 4, 2), ALL)
    vocab = ("y", "z", "c")
    in_specs = (P("x", None), P("x", vocab), P(ALL, None), P(None, vocab, "x"))
    out_specs = (P(), P(ALL, None), P(None, vocab, "x"))
    return jax.shard_map(shards, mesh=mesh, in_specs=in_specs, out_specs=out_specs, check_vma=False)
```

```python
import functools

import jax
import jax.numpy as jnp
import numpy as np
from jax import lax
from jax.experimental import pallas as pl
from jax.experimental.pallas import tpu as pltpu
from jax.sharding import Mesh
from jax.sharding import PartitionSpec as P

grad_scale = 64.0
ROWS = (8, 4)
ALL = ("x", "y", "z", "c")
CHIPS = ("x", "y", "z")
SWAP = [(0, 1), (1, 0)]
F32, BF16 = jnp.float32, jnp.bfloat16
NT = (((1,), (1,)), ((), ()))
TN = (((0,), (0,)), ((), ()))
MIB = 2**20


def shift(k):
    return [(i, (i + k) % 4) for i in range(4)]


def dot(a, b, dims=(((1,), (0,)), ((), ()))):
    return lax.dot_general(a, b, dims, preferred_element_type=F32)


def call(body, scalars, args, in_specs, outs, out_specs, grid=(1,), flops=0, after=(), spare=4, scratch=()):
    n = 1 + len(args)
    blocks = [(s.block_shape or (), a.dtype) for s, a in zip([*in_specs, *out_specs], [*args, *outs])]
    held = sum(int(np.prod(shape)) * dtype.itemsize for shape, dtype in blocks) * (1 if grid == (1,) else 2)

    def ordered(*refs):
        body(*refs[:n], *refs[n + len(after) :])

    return pl.pallas_call(
        ordered if after else body,
        out_shape=outs,
        grid_spec=pltpu.PrefetchScalarGridSpec(
            num_scalar_prefetch=1,
            grid=grid,
            in_specs=list(in_specs) + [pl.BlockSpec(memory_space=pl.ANY)] * len(after),
            out_specs=out_specs,
            scratch_shapes=scratch,
        ),
        compiler_params=pltpu.CompilerParams(vmem_limit_bytes=held + spare * MIB),
        cost_estimate=pl.CostEstimate(flops=flops, bytes_accessed=0, transcendentals=0),
    )(scalars, *args, *after)


def whole(shape):
    return pl.BlockSpec(shape, lambda *_: (0,) * len(shape))


def sds(shape, dtype):
    return jax.ShapeDtypeStruct(shape, dtype)


def cut_body(where, th, sh, own, s1, s2, s3):
    ks = th.shape[1] // 4
    x, c = where[0], where[1]
    def block(k):
        return th[:, pl.ds(pl.multiple_of(lax.rem(x + k, 4) * ks, ks), ks)]

    def one_hot(part, of):
        picks = []
        for m, start in zip(ROWS, (0, ROWS[0])):
            n = 16 * m // of
            i = lax.broadcasted_iota(jnp.int32, (n, th.shape[0]), 0) + part * n
            chip = lax.shift_right_logical(i, m.bit_length() - 1)
            row = chip * sum(ROWS) + start + jnp.bitwise_and(i, m - 1)
            picks.append(jnp.where(row == lax.broadcasted_iota(jnp.int32, row.shape, 1), 1.0, 0.0))
        return jnp.concatenate(picks, axis=0).astype(BF16)

    pick = one_hot(c, 2)
    for k, out in ((1, s1), (2, s2), (3, s3)):
        n = pick.shape[0]
        out[:n, :] = dot(pick, block(k)).astype(BF16)
        out[n:, :] = jnp.zeros((16, ks), BF16)
        m, d = sh.shape
        out[n : n + m, :] = sh[:, :ks]
        out[n + 8 : n + 8 + m, : d - ks] = sh[:, ks:]
    own[...] = dot(one_hot(0, 1), block(0)).astype(BF16)


def cut(where, th, sh):
    rows, d = th.shape
    ks = d // 4
    outs = [sds((rows, ks), BF16)] + [sds((rows // 2 + 16, ks), BF16)] * 3
    return call(
        cut_body, where, (th, sh), [whole(th.shape), whole(sh.shape)], outs, [whole(o.shape) for o in outs],
        flops=4 * rows * rows * d, spare=8,
    )


def pad_body(where, sh, out):
    out[...] = jnp.zeros_like(out)
    out[: sh.shape[0], :] = sh[...]


def pad_rows(where, sh):
    out = sds((8, sh.shape[1]), BF16)
    return call(pad_body, where, (sh,), [whole(sh.shape)], [out], [whole(out.shape)])[0]


def stack_body(piece, where, s0, g1, g2, g3, t0, o1, o2, o3, out, held):
    ks = g1.shape[1]
    at = 0
    for first, rest in ((s0, (g1, g2, g3)), (t0, (o1, o2, o3))):
        held[at : at + 8, :] = first[...]
        for k, ref in enumerate(rest):
            n = ref.shape[0] - 16
            to = at + 8 * k + 8
            held[to : to + 8, :ks] = ref[n : n + 8, :]
            held[to : to + 8, ks:] = ref[n + 8 :, : out.shape[1] - ks]
        at += 32
    row = lax.broadcasted_iota(jnp.int32, (out.shape[0], 64), 0)
    block = lax.shift_right_logical(row * 43, 8)
    source = row + (8 - piece) * block
    pick = jnp.where(source == lax.broadcasted_iota(jnp.int32, source.shape, 1), 1.0, 0.0).astype(BF16)
    out[...] = dot(pick, held[...]).astype(BF16)


def stack(where, piece, *pieces):
    d = pieces[0].shape[1]
    out = sds((8 * piece, d), BF16)
    specs = [whole(p.shape) for p in pieces]
    body = functools.partial(stack_body, piece)
    return call(body, where, pieces, specs, [out], [whole(out.shape)], scratch=[pltpu.VMEM((64, d), BF16)])[0]


def pick_body(piece, where, out):
    x, c = where[0], where[1]
    n = 64 * ROWS[0]
    for at, count, m, start in ((0, n, ROWS[0], 0), (n, 64 * ROWS[1], ROWS[1], ROWS[0])):
        i = lax.broadcasted_iota(jnp.int32, (count, 1), 0)
        bits = m.bit_length() - 1
        row = start + jnp.bitwise_and(i, m - 1)
        chip = jnp.bitwise_and(lax.shift_right_logical(i, bits), 15)
        k = jnp.bitwise_and(x + 4 - lax.shift_right_logical(i, bits + 4), 3)
        late = jnp.where(row >= piece, 1, 0)
        source = chip * (8 * piece) + jnp.where(late != c, 4 * piece, 0) + k * piece + row - piece * late
        col = lax.broadcasted_iota(jnp.int32, (count, out.shape[1]), 1)
        out[at : at + count, :] = jnp.where(col == source, 1.0, 0.0).astype(BF16)


def pick_of(where, piece, after):
    tokens = 64 * sum(ROWS)
    out = sds((tokens, tokens), BF16)
    body = functools.partial(pick_body, piece)
    return call(body, where, (), [], [out], [whole(out.shape)], after=after, spare=8)[0]


def columns(where, tw, step):
    n = tw.shape[1] // 4
    return tw[:, pl.ds(pl.multiple_of(lax.rem(where[0] + step, 4) * n, n), n)]


def gather_body(where, own, g1, g2, g3, o1, o2, o3, h):
    x, c = where[0], where[1]
    for m, start in zip(ROWS, (0, ROWS[0])):
        n = 16 * m
        nh = n // 2
        base, at = 64 * start, 16 * start
        h[pl.ds(pl.multiple_of(base + x * n, nh), n), :] = own[at : at + n, :]
        at = at // 2
        for k, (a, b) in enumerate(((g1, o1), (g2, o2), (g3, o3))):
            to = base + lax.rem(x + 3 - k, 4) * n
            h[pl.ds(pl.multiple_of(to + c * nh, nh), nh), :] = a[at : at + nh, :]
            h[pl.ds(pl.multiple_of(to + (1 - c) * nh, nh), nh), :] = b[at : at + nh, :]


def gather(where, own, got, other):
    out = sds((4 * own.shape[0], own.shape[1]), BF16)
    args = (own, *got, *other)
    return call(gather_body, where, args, [whole(a.shape) for a in args], [out], [whole(out.shape)])[0]


def rest_body(where, h, tw, out):
    half = h.shape[0] // 2
    out[0] = dot(h[...], columns(where, tw, 2))
    out[1, :half, :] = dot(h[:half, :], columns(where, tw, 1))
    out[1, half:, :] = dot(h[half:, :], columns(where, tw, 3))
    out[2] = dot(h[...], columns(where, tw, 0))


def rest(where, h, tw):
    rows, ks = h.shape
    cols = tw.shape[1] // 4
    out = sds((3, rows, cols), F32)
    specs = [whole(h.shape), whole(tw.shape)]
    return call(rest_body, where, (h, tw), specs, [out], [whole(out.shape)], flops=6 * rows * ks * cols, spare=6)[0]


def hop_body(where, p, right, left, r, l):
    half = right.shape[0]
    r[...] = p[0, :half, :] + right[...]
    l[...] = p[0, half:, :] + left[...]


def hop(where, p, step, right, left):
    half, cols = right.shape
    out = sds(right.shape, F32)
    specs = [pl.BlockSpec((1, 2 * half, cols), lambda i, w: (step, 0, 0)), whole(right.shape), whole(left.shape)]
    return call(hop_body, where, (p, right, left), specs, [out, out], [whole(out.shape)] * 2)


def student_body(where, pick, rows, w, hs, sl):
    block = dot(pick[...], rows[...]).astype(BF16)
    hs[...] = block

    @pl.when(pl.program_id(0) == 0)
    def _():
        sl[...] = jnp.zeros_like(sl)

    sl[...] += dot(block, w[...])


def student(where, pick, rows, w, after):
    tokens, room = pick.shape
    d, cols = w.shape
    tile = d // 6
    specs = [
        whole(pick.shape),
        pl.BlockSpec((room, tile), lambda i, s: (0, i)),
        pl.BlockSpec((tile, cols), lambda i, s: (i, 0)),
    ]
    outs = [sds((tokens, d), BF16), sds((tokens, cols), F32)]
    return call(
        student_body, where, (pick, rows, w), specs, outs,
        [pl.BlockSpec((tokens, tile), lambda i, s: (0, i)), whole(outs[1].shape)],
        grid=(6,), flops=2 * tokens * d * (room + cols), after=after, spare=6,
    )


def local_body(where, p, rr, lr, sl, tl, st):
    half, cols = rr.shape
    tl[:half, :] = p[0, :half, :] + rr[...]
    tl[half:, :] = p[0, half:, :] + lr[...]
    t, s = tl[...], sl[...]
    t_max = jnp.max(t, axis=1, keepdims=True)
    s_max = jnp.max(s, axis=1, keepdims=True)
    te = jnp.exp(t - t_max)
    t_sum = jnp.sum(te, axis=1, keepdims=True)
    cross = jnp.sum(te * (t - s), axis=1, keepdims=True)
    s_sum = jnp.sum(jnp.exp(s - s_max), axis=1, keepdims=True)
    lane = lax.broadcasted_iota(jnp.int32, (2 * half, 128), 1)
    packed = jnp.zeros((2 * half, 128), F32)
    for i, v in enumerate((t_max, t_sum, cross, s_max, s_sum)):
        packed = jnp.where(lane == i, v, packed)
    st[...] = jnp.transpose(packed)[:8, :]


def local(where, p, right, left, sl):
    outs = [sds(sl.shape, F32), sds((8, sl.shape[0]), F32)]
    args = (p, right, left, sl)
    specs = [pl.BlockSpec((1,) + sl.shape, lambda i, s: (2, 0, 0))] + [whole(a.shape) for a in args[1:]]
    return call(local_body, where, args, specs, outs, [whole(o.shape) for o in outs], flops=40 * sl.size, spare=10)


def merged(i, pieces):
    n = len(pieces)
    ordered = []
    for j in range(n):
        v = pieces[0]
        for k in range(1, n):
            v = jnp.where(lax.rem(i - j + n, n) == k, pieces[k], v)
        ordered.append(v)
    t_max = functools.reduce(jnp.maximum, [v[0:1] for v in ordered])
    s_max = functools.reduce(jnp.maximum, [v[3:4] for v in ordered])
    t_w = [jnp.exp(v[0:1] - t_max) for v in ordered]
    s_w = [jnp.exp(v[3:4] - s_max) for v in ordered]
    t_sum = sum(v[1:2] * a for v, a in zip(ordered, t_w))
    cross = sum(v[2:3] * a for v, a in zip(ordered, t_w))
    s_sum = sum(v[4:5] * a for v, a in zip(ordered, s_w))
    return [t_max, t_sum, cross, s_max, s_sum]


def merge_body(axis, where, *refs):
    pieces = [r[...] for r in refs[:-1]]
    rows = merged(where[axis], pieces)
    refs[-1][...] = jnp.concatenate(rows + [jnp.zeros_like(pieces[0][:3])], axis=0)


def merge(where, axis, *pieces):
    shape = pieces[0].shape
    body = functools.partial(merge_body, axis)
    return call(body, where, pieces, [whole(shape)] * len(pieces), [sds(shape, F32)], [whole(shape)])[0]


def back(grad, place, w):
    n = 64 * ROWS[0]
    half = w.shape[0] // 2
    b = grad[n:, :]
    low = dot(dot(place[0], b).astype(BF16), w[:half, :], NT)
    low += dot(dot(place[1], b).astype(BF16), w[half:, :], NT)
    return dot(grad[:n, :], w[...], NT), low


def grad_body(where, own, g1, g2, g3, tl, sl, place, w, g, away, kl):
    t_max, t_sum, cross, s_max, s_sum = merged(where[0], [own[...], g1[...], g2[...], g3[...]])
    rows = cross / t_sum - t_max - jnp.log(t_sum) + s_max + jnp.log(s_sum)
    kl[0, 0] = jnp.sum(rows) / rows.shape[1]
    stats = jnp.concatenate([t_max, grad_scale / t_sum, s_max, grad_scale / s_sum], axis=0)
    stats = jnp.concatenate([stats, jnp.zeros((124, stats.shape[1]), F32)], axis=0)
    cols = jnp.transpose(stats)
    s = jnp.exp(sl[...] - cols[:, 2:3]) * cols[:, 3:4]
    g[...] = (s - jnp.exp(tl[...] - cols[:, 0:1]) * cols[:, 1:2]).astype(BF16)
    split = w.shape[0]
    a, b = back(g[...], place, w)
    away[:, :split] = a.astype(BF16)
    away[:, split:] = b.astype(BF16)


def grad_of(where, pieces, tl, sl, place, w):
    tokens, cols = sl.shape
    d = w.shape[0]
    outs = [sds((tokens, cols), BF16), sds((512, d // 4 * 3), BF16), sds((1, 1), F32)]
    args = (*pieces, tl, sl, place, w)
    specs = [whole(a.shape) for a in args[:-1]] + [pl.BlockSpec((d // 2, cols), lambda i, s: (1 - s[1], 0))]
    out_specs = [whole(o.shape) for o in outs[:2]] + [pl.BlockSpec(memory_space=pltpu.SMEM)]
    return call(grad_body, where, args, specs, outs, out_specs, flops=tokens * cols * d, spare=16)


def keep_body(where, g, place, w, out):
    split = w.shape[0]
    a, b = back(g[...], place, w)
    out[:, :split] = a
    out[:, split:] = b


def keep_of(where, g, place, w):
    tokens, cols = g.shape
    d = w.shape[0]
    out = sds((512, d // 4 * 3), F32)
    specs = [whole(g.shape), whole(place.shape), pl.BlockSpec((d // 2, cols), lambda i, s: (s[1], 0))]
    return call(keep_body, where, (g, place, w), specs, [out], [whole(out.shape)], flops=tokens * cols * d, spare=12)[0]


def add_body(where, kept, got, out):
    out[...] = (kept[...] + got[...].astype(F32)).astype(BF16)


def add(where, kept, got):
    specs = [whole(kept.shape)] * 2
    return call(add_body, where, (kept, got), specs, [sds(kept.shape, BF16)], [whole(kept.shape)], spare=6)[0]


def total_body(where, parts, mine, theirs):
    both = jnp.sum(parts[...].astype(F32), axis=0)
    half = both.shape[1] // 3
    a, b = both[:, : 2 * half], both[:, 2 * half :]
    n = sum(ROWS) // 2
    late = jnp.concatenate([b[: ROWS[1]], b[ROWS[1] :]], axis=1)
    second = jnp.concatenate([a[n:], late, jnp.zeros_like(a[n:])], axis=0)
    mine[...] = jnp.where(where[1] == 0, a, second).astype(BF16)
    theirs[...] = jnp.where(where[1] == 0, second, a).astype(BF16)


def total(where, parts, after):
    out = sds((8, parts.shape[2] // 3 * 2), BF16)
    return call(total_body, where, (parts,), [whole(parts.shape)], [out, out], [whole(out.shape)] * 2, after=after, spare=10)


def join_body(where, mine, got, out):
    half = mine.shape[1]
    n = out.shape[0]
    out[:, pl.ds(pl.multiple_of(where[1] * half, half), half)] = mine[:n, :]
    out[:, pl.ds(pl.multiple_of((1 - where[1]) * half, half), half)] = got[:n, :]


def join(where, mine, got, shape):
    return call(join_body, where, (mine, got), [whole(mine.shape)] * 2, [sds(shape, BF16)], [whole(shape)])[0]


def weight_body(where, hs, g, out, done):
    out[...] = dot(hs[...], g[...], TN)[:, None, :]
    done[...] = jnp.zeros_like(done)


def weight_of(where, hs, g, after):
    tokens, d = hs.shape
    cols = g.shape[1]
    tile = 256
    outs = [sds((d, 1, cols), F32), sds((8, 128), F32)]
    specs = [pl.BlockSpec((tokens, tile), lambda i, s: (0, i)), whole(g.shape)]
    return call(
        weight_body, where, (hs, g), specs, outs,
        [pl.BlockSpec((tile, 1, cols), lambda i, s: (i, 0, 0)), whole((8, 128))],
        grid=(d // tile,), flops=2 * tokens * d * cols, after=after,
    )


def place_of(m):
    place = np.zeros((2, 64, 2, m, 64, m), np.float32)
    for chip in range(64):
        for r in range(m):
            for h in range(2):
                place[h, chip, h, r, chip, r] = 1.0
    return jnp.asarray(place.reshape(2, 128 * m, 64 * m), BF16)


def shards(th, tw, sh, sw):
    x = lax.axis_index("x")
    where = jnp.stack([lax.axis_index(a) for a in ("x", "c", "y", "z")]).astype(jnp.int32)
    piece = sh.shape[0]
    w = sw[:, 0, :]
    place = place_of(ROWS[1])

    def both_ways(r, l):
        return lax.ppermute(r, "x", shift(1)), lax.ppermute(l, "x", shift(-1))

    def others(v, axis):
        return [lax.ppermute(v, axis, shift(k)) for k in (1, 2, 3)]

    def swap(v):
        return lax.ppermute(v, "c", SWAP)

    own, *sends = cut(where, th, sh)
    got = [lax.ppermute(s, "x", shift(k + 1)) for k, s in enumerate(sends)]
    other = [swap(v) for v in got]

    sh8 = pad_rows(where, sh)
    every = lax.all_gather(stack(where, piece, sh8, *got, swap(sh8), *other), ("y", "z"), axis=0, tiled=True)
    h = gather(where, own, got, other)
    cols = tw.shape[1] // 4

    def product(rows, step):
        block = lax.dynamic_slice(tw, (0, (x + step) % 4 * cols), (tw.shape[0], cols))
        return jnp.dot(rows, block, preferred_element_type=F32)

    half = h.shape[0] // 2
    right, left = both_ways(product(h[:half], 3), product(h[half:], 1))
    p = rest(where, h, tw)
    r, l = hop(where, p, 0, right, left)
    right, left = both_ways(r, l)
    r, l = hop(where, p, 1, right, left)
    right, left = both_ways(r, l)
    pick = pick_of(where, piece, (p,))
    hs, sl = student(where, pick, every, w, (r,))
    tl, st = local(where, p, right, left, sl)

    st = merge(where, 1, st, swap(st))
    st = merge(where, 3, st, *others(st, "z"))
    st = merge(where, 2, st, *others(st, "y"))
    grad, away, kl = grad_of(where, [st, *others(st, "x")], tl, sl, place, w)
    got = swap(away)
    chip = add(where, keep_of(where, grad, place, w), got)
    parts = lax.all_to_all(chip.reshape(64, 8, -1), CHIPS, split_axis=0, concat_axis=0, tiled=True)
    grad_weight, done = weight_of(where, hs, grad, (chip,))
    mine, theirs = total(where, parts, (done,))
    grad_hidden = join(where, mine, swap(theirs), sh.shape)
    return (kl.reshape(()), grad_hidden, grad_weight)


def solution(mesh):
    mesh = Mesh(mesh.devices.reshape(4, 4, 4, 2), ALL)
    vocab = ("y", "z", "c")
    in_specs = (P("x", None), P("x", vocab), P(ALL, None), P(None, vocab, "x"))
    out_specs = (P(), P(ALL, None), P(None, vocab, "x"))
    return jax.shard_map(shards, mesh=mesh, in_specs=in_specs, out_specs=out_specs, check_vma=False)
```

```python
import functools

import jax
import jax.numpy as jnp
import numpy as np
from jax import lax
from jax.experimental import pallas as pl
from jax.experimental.pallas import tpu as pltpu
from jax.sharding import Mesh
from jax.sharding import PartitionSpec as P

grad_scale = 64.0
ROWS = (8, 4)
ALL = ("x", "y", "z", "c")
CHIPS = ("x", "y", "z")
SWAP = [(0, 1), (1, 0)]
F32, BF16 = jnp.float32, jnp.bfloat16
NT = (((1,), (1,)), ((), ()))
TN = (((0,), (0,)), ((), ()))
MIB = 2**20


def shift(k):
    return [(i, (i + k) % 4) for i in range(4)]


def dot(a, b, dims=(((1,), (0,)), ((), ()))):
    return lax.dot_general(a, b, dims, preferred_element_type=F32)


def call(body, scalars, args, in_specs, outs, out_specs, grid=(1,), flops=0, after=(), spare=4, scratch=()):
    n = 1 + len(args)
    blocks = [(s.block_shape or (), a.dtype) for s, a in zip([*in_specs, *out_specs], [*args, *outs])]
    held = sum(int(np.prod(shape)) * dtype.itemsize for shape, dtype in blocks) * (1 if grid == (1,) else 2)

    def ordered(*refs):
        body(*refs[:n], *refs[n + len(after) :])

    return pl.pallas_call(
        ordered if after else body,
        out_shape=outs,
        grid_spec=pltpu.PrefetchScalarGridSpec(
            num_scalar_prefetch=1,
            grid=grid,
            in_specs=list(in_specs) + [pl.BlockSpec(memory_space=pl.ANY)] * len(after),
            out_specs=out_specs,
            scratch_shapes=scratch,
        ),
        compiler_params=pltpu.CompilerParams(vmem_limit_bytes=held + spare * MIB),
        cost_estimate=pl.CostEstimate(flops=flops, bytes_accessed=0, transcendentals=0),
    )(scalars, *args, *after)


def whole(shape):
    return pl.BlockSpec(shape, lambda *_: (0,) * len(shape))


def sds(shape, dtype):
    return jax.ShapeDtypeStruct(shape, dtype)


def cut_body(where, th, sh, own, s1, s2, s3, sh8):
    ks = th.shape[1] // 4
    x, c = where[0], where[1]
    def block(k):
        return th[:, pl.ds(pl.multiple_of(lax.rem(x + k, 4) * ks, ks), ks)]

    def one_hot(part, of):
        picks = []
        for m, start in zip(ROWS, (0, ROWS[0])):
            n = 16 * m // of
            i = lax.broadcasted_iota(jnp.int32, (n, th.shape[0]), 0) + part * n
            chip = lax.shift_right_logical(i, m.bit_length() - 1)
            row = chip * sum(ROWS) + start + jnp.bitwise_and(i, m - 1)
            picks.append(jnp.where(row == lax.broadcasted_iota(jnp.int32, row.shape, 1), 1.0, 0.0))
        return jnp.concatenate(picks, axis=0).astype(BF16)

    pick = one_hot(c, 2)
    for k, out in ((1, s1), (2, s2), (3, s3)):
        n = pick.shape[0]
        out[:n, :] = dot(pick, block(k)).astype(BF16)
        out[n:, :] = jnp.zeros((16, ks), BF16)
        m, d = sh.shape
        out[n : n + m, :] = sh[:, :ks]
        out[n + 8 : n + 8 + m, : d - ks] = sh[:, ks:]
    own[...] = dot(one_hot(0, 1), block(0)).astype(BF16)
    sh8[...] = jnp.zeros_like(sh8)
    sh8[: sh.shape[0], :] = sh[...]


def cut(where, th, sh):
    rows, d = th.shape
    ks = d // 4
    outs = [sds((rows, ks), BF16)] + [sds((rows // 2 + 16, ks), BF16)] * 3 + [sds((8, sh.shape[1]), BF16)]
    return call(
        cut_body, where, (th, sh), [whole(th.shape), whole(sh.shape)], outs, [whole(o.shape) for o in outs],
        flops=4 * rows * rows * d, spare=8,
    )


def stack_body(piece, where, s0, g1, g2, g3, out, held):
    ks = g1.shape[1]
    held[:8, :] = s0[...]
    for k, ref in enumerate((g1, g2, g3)):
        n = ref.shape[0] - 16
        to = 8 * k + 8
        held[to : to + 8, :ks] = ref[n : n + 8, :]
        held[to : to + 8, ks:] = ref[n + 8 :, : out.shape[1] - ks]
    row = lax.broadcasted_iota(jnp.int32, (out.shape[0], 32), 0)
    source = row
    for k in (1, 2, 3):
        source += jnp.where(row >= k * piece, 8 - piece, 0)
    pick = jnp.where(source == lax.broadcasted_iota(jnp.int32, source.shape, 1), 1.0, 0.0).astype(BF16)
    out[...] = dot(pick, held[...]).astype(BF16)


def stack(where, piece, *pieces):
    d = pieces[0].shape[1]
    out = sds((4 * piece, d), BF16)
    specs = [whole(p.shape) for p in pieces]
    body = functools.partial(stack_body, piece)
    return call(body, where, pieces, specs, [out], [whole(out.shape)], scratch=[pltpu.VMEM((32, d), BF16)])[0]


def pick_body(piece, where, out):
    x = where[0]
    n = 64 * ROWS[0]
    for at, count, m, start in ((0, n, ROWS[0], 0), (n, 64 * ROWS[1], ROWS[1], ROWS[0])):
        i = lax.broadcasted_iota(jnp.int32, (count, 1), 0)
        bits = m.bit_length() - 1
        row = start + jnp.bitwise_and(i, m - 1)
        chip = jnp.bitwise_and(lax.shift_right_logical(i, bits), 15)
        k = jnp.bitwise_and(x + 4 - lax.shift_right_logical(i, bits + 4), 3)
        late = jnp.where(row >= piece, 1, 0)
        source = chip * (8 * piece) + late * (4 * piece) + k * piece + row - piece * late
        col = lax.broadcasted_iota(jnp.int32, (count, out.shape[1]), 1)
        out[at : at + count, :] = jnp.where(col == source, 1.0, 0.0).astype(BF16)


def pick_of(where, piece, after):
    tokens = 64 * sum(ROWS)
    out = sds((tokens, tokens), BF16)
    body = functools.partial(pick_body, piece)
    return call(body, where, (), [], [out], [whole(out.shape)], after=after, spare=8)[0]


def columns(where, tw, step):
    n = tw.shape[1] // 4
    return tw[:, pl.ds(pl.multiple_of(lax.rem(where[0] + step, 4) * n, n), n)]


def gather_body(where, own, g1, g2, g3, o1, o2, o3, h):
    x, c = where[0], where[1]
    for m, start in zip(ROWS, (0, ROWS[0])):
        n = 16 * m
        nh = n // 2
        base, at = 64 * start, 16 * start
        h[pl.ds(pl.multiple_of(base + x * n, nh), n), :] = own[at : at + n, :]
        at = at // 2
        for k, (a, b) in enumerate(((g1, o1), (g2, o2), (g3, o3))):
            to = base + lax.rem(x + 3 - k, 4) * n
            h[pl.ds(pl.multiple_of(to + c * nh, nh), nh), :] = a[at : at + nh, :]
            h[pl.ds(pl.multiple_of(to + (1 - c) * nh, nh), nh), :] = b[at : at + nh, :]


def gather(where, own, got, other):
    out = sds((4 * own.shape[0], own.shape[1]), BF16)
    args = (own, *got, *other)
    return call(gather_body, where, args, [whole(a.shape) for a in args], [out], [whole(out.shape)])[0]


def rest_body(where, h, tw, out):
    half = h.shape[0] // 2
    out[0] = dot(h[...], columns(where, tw, 2))
    out[1, :half, :] = dot(h[:half, :], columns(where, tw, 1))
    out[1, half:, :] = dot(h[half:, :], columns(where, tw, 3))
    out[2] = dot(h[...], columns(where, tw, 0))


def rest(where, h, tw):
    rows, ks = h.shape
    cols = tw.shape[1] // 4
    out = sds((3, rows, cols), F32)
    specs = [whole(h.shape), whole(tw.shape)]
    return call(rest_body, where, (h, tw), specs, [out], [whole(out.shape)], flops=6 * rows * ks * cols, spare=6)[0]


def hop_body(where, pr, pl_, right, left, r, l):
    r[...] = pr[0] + right[...]
    l[...] = pl_[0] + left[...]


def hop(where, p, step, i, right, left, after=(), flops=0):
    n, cols = right.shape
    out = sds(right.shape, F32)
    specs = [pl.BlockSpec((1, n, cols), lambda _, w, j=j: (step, j, 0)) for j in (i, i + 2)]
    specs += [whole(right.shape), whole(left.shape)]
    return call(hop_body, where, (p, p, right, left), specs, [out, out], [whole(out.shape)] * 2, after=after, flops=flops)


def student_body(where, pick, rows, w, sl, total):
    @pl.when(pl.program_id(0) == 0)
    def _():
        total[...] = jnp.zeros_like(total)

    total[...] += dot(rows[...], w[...])

    @pl.when(pl.program_id(0) == pl.num_programs(0) - 1)
    def _():
        rest = total[...]
        out = jnp.zeros_like(rest)
        for _ in range(3):
            part = rest.astype(BF16)
            out += dot(pick[...], part)
            rest -= part.astype(F32)
        sl[...] = out


def student(where, pick, rows, w, after):
    tokens, d = rows.shape
    cols = w.shape[1]
    tile = d // 6
    specs = [
        whole(pick.shape),
        pl.BlockSpec((tokens, tile), lambda i, s: (0, i)),
        pl.BlockSpec((tile, cols), lambda i, s: (i, 0)),
    ]
    out = sds((tokens, cols), F32)
    return call(
        student_body, where, (pick, rows, w), specs, [out], [whole(out.shape)],
        grid=(6,), after=after, spare=8, scratch=[pltpu.VMEM(out.shape, F32)],
    )[0]


def local_body(where, p, r0, l0, r1, l1, sl, tl, st):
    n = r0.shape[0]
    half = 2 * n
    tl[:n, :] = r0[...]
    tl[2 * n : 3 * n, :] = l0[...]
    tl[n : 2 * n, :] = p[0, n : 2 * n, :] + r1[...]
    tl[3 * n :, :] = p[0, 3 * n :, :] + l1[...]
    t, s = tl[...], sl[...]
    t_max = jnp.max(t, axis=1, keepdims=True)
    s_max = jnp.max(s, axis=1, keepdims=True)
    te = jnp.exp(t - t_max)
    t_sum = jnp.sum(te, axis=1, keepdims=True)
    cross = jnp.sum(te * (t - s), axis=1, keepdims=True)
    s_sum = jnp.sum(jnp.exp(s - s_max), axis=1, keepdims=True)
    lane = lax.broadcasted_iota(jnp.int32, (2 * half, 128), 1)
    packed = jnp.zeros((2 * half, 128), F32)
    for i, v in enumerate((t_max, t_sum, cross, s_max, s_sum)):
        packed = jnp.where(lane == i, v, packed)
    st[...] = jnp.transpose(packed)[:8, :]


def local(where, p, chains, sl):
    outs = [sds(sl.shape, F32), sds((8, sl.shape[0]), F32)]
    args = (p, *chains, sl)
    specs = [pl.BlockSpec((1,) + sl.shape, lambda i, s: (2, 0, 0))] + [whole(a.shape) for a in args[1:]]
    return call(local_body, where, args, specs, outs, [whole(o.shape) for o in outs], flops=40 * sl.size, spare=10)


def merged(i, pieces):
    n = len(pieces)
    ordered = []
    for j in range(n):
        v = pieces[0]
        for k in range(1, n):
            v = jnp.where(lax.rem(i - j + n, n) == k, pieces[k], v)
        ordered.append(v)
    t_max = functools.reduce(jnp.maximum, [v[0:1] for v in ordered])
    s_max = functools.reduce(jnp.maximum, [v[3:4] for v in ordered])
    t_w = [jnp.exp(v[0:1] - t_max) for v in ordered]
    s_w = [jnp.exp(v[3:4] - s_max) for v in ordered]
    t_sum = sum(v[1:2] * a for v, a in zip(ordered, t_w))
    cross = sum(v[2:3] * a for v, a in zip(ordered, t_w))
    s_sum = sum(v[4:5] * a for v, a in zip(ordered, s_w))
    return [t_max, t_sum, cross, s_max, s_sum]


def merge_body(axis, where, *refs):
    pieces = [r[...] for r in refs[:-1]]
    rows = merged(where[axis], pieces)
    refs[-1][...] = jnp.concatenate(rows + [jnp.zeros_like(pieces[0][:3])], axis=0)


def merge(where, axis, *pieces):
    shape = pieces[0].shape
    body = functools.partial(merge_body, axis)
    return call(body, where, pieces, [whole(shape)] * len(pieces), [sds(shape, F32)], [whole(shape)])[0]


def back(grad, place, w):
    n = 64 * ROWS[0]
    half = w.shape[0] // 2
    b = grad[n:, :]
    low = dot(dot(place[0], b).astype(BF16), w[:half, :], NT)
    low += dot(dot(place[1], b).astype(BF16), w[half:, :], NT)
    return dot(grad[:n, :], w[...], NT), low


def grad_body(where, own, g1, g2, g3, tl, sl, place, w, g, away, kl):
    t_max, t_sum, cross, s_max, s_sum = merged(where[0], [own[...], g1[...], g2[...], g3[...]])
    rows = cross / t_sum - t_max - jnp.log(t_sum) + s_max + jnp.log(s_sum)
    kl[0, 0] = jnp.sum(rows) / rows.shape[1]
    stats = jnp.concatenate([t_max, grad_scale / t_sum, s_max, grad_scale / s_sum], axis=0)
    stats = jnp.concatenate([stats, jnp.zeros((124, stats.shape[1]), F32)], axis=0)
    cols = jnp.transpose(stats)
    s = jnp.exp(sl[...] - cols[:, 2:3]) * cols[:, 3:4]
    g[...] = (s - jnp.exp(tl[...] - cols[:, 0:1]) * cols[:, 1:2]).astype(BF16)
    split = w.shape[0]
    a, b = back(g[...], place, w)
    away[:, :split] = a.astype(BF16)
    away[:, split:] = b.astype(BF16)


def grad_of(where, pieces, tl, sl, place, w):
    tokens, cols = sl.shape
    d = w.shape[0]
    outs = [sds((tokens, cols), BF16), sds((512, d // 4 * 3), BF16), sds((1, 1), F32)]
    args = (*pieces, tl, sl, place, w)
    specs = [whole(a.shape) for a in args[:-1]] + [pl.BlockSpec((d // 2, cols), lambda i, s: (1 - s[1], 0))]
    out_specs = [whole(o.shape) for o in outs[:2]] + [pl.BlockSpec(memory_space=pltpu.SMEM)]
    return call(grad_body, where, args, specs, outs, out_specs, flops=tokens * cols * d, spare=16)


def keep_body(where, g, place, w, out):
    split = w.shape[0]
    a, b = back(g[...], place, w)
    out[:, :split] = a
    out[:, split:] = b


def keep_of(where, g, place, w):
    tokens, cols = g.shape
    d = w.shape[0]
    out = sds((512, d // 4 * 3), F32)
    specs = [whole(g.shape), whole(place.shape), pl.BlockSpec((d // 2, cols), lambda i, s: (s[1], 0))]
    return call(keep_body, where, (g, place, w), specs, [out], [whole(out.shape)], flops=tokens * cols * d, spare=12)[0]


def add_body(where, kept, got, out):
    out[...] = (kept[...] + got[...].astype(F32)).astype(BF16)


def add(where, kept, got):
    specs = [whole(kept.shape)] * 2
    return call(add_body, where, (kept, got), specs, [sds(kept.shape, BF16)], [whole(kept.shape)], spare=6)[0]


def total_body(where, parts, mine, theirs):
    both = jnp.sum(parts[...].astype(F32), axis=0)
    half = both.shape[1] // 3
    a, b = both[:, : 2 * half], both[:, 2 * half :]
    n = sum(ROWS) // 2
    late = jnp.concatenate([b[: ROWS[1]], b[ROWS[1] :]], axis=1)
    second = jnp.concatenate([a[n:], late, jnp.zeros_like(a[n:])], axis=0)
    mine[...] = jnp.where(where[1] == 0, a, second).astype(BF16)
    theirs[...] = jnp.where(where[1] == 0, second, a).astype(BF16)


def total(where, parts, after):
    out = sds((8, parts.shape[2] // 3 * 2), BF16)
    return call(total_body, where, (parts,), [whole(parts.shape)], [out, out], [whole(out.shape)] * 2, after=after, spare=10)


def join_body(where, mine, got, out):
    half = mine.shape[1]
    n = out.shape[0]
    out[:, pl.ds(pl.multiple_of(where[1] * half, half), half)] = mine[:n, :]
    out[:, pl.ds(pl.multiple_of((1 - where[1]) * half, half), half)] = got[:n, :]


def join(where, mine, got, shape):
    return call(join_body, where, (mine, got), [whole(mine.shape)] * 2, [sds(shape, BF16)], [whole(shape)])[0]


def weight_body(where, rows, g, pick, out, done, placed):
    @pl.when(pl.program_id(0) == 0)
    def _():
        placed[...] = dot(pick[...], g[...], TN).astype(BF16)

    out[...] = dot(rows[...], placed[...], TN)[:, None, :]
    done[...] = jnp.zeros_like(done)


def weight_of(where, rows, g, pick, after):
    tokens, d = rows.shape
    cols = g.shape[1]
    tile = 256
    outs = [sds((d, 1, cols), F32), sds((8, 128), F32)]
    specs = [pl.BlockSpec((tokens, tile), lambda i, s: (0, i)), whole(g.shape), whole(pick.shape)]
    return call(
        weight_body, where, (rows, g, pick), specs, outs,
        [pl.BlockSpec((tile, 1, cols), lambda i, s: (i, 0, 0)), whole((8, 128))],
        grid=(d // tile,), flops=2 * tokens * d * cols, after=after, scratch=[pltpu.VMEM(g.shape, BF16)],
    )


def place_of(m):
    place = np.zeros((2, 64, 2, m, 64, m), np.float32)
    for chip in range(64):
        for r in range(m):
            for h in range(2):
                place[h, chip, h, r, chip, r] = 1.0
    return jnp.asarray(place.reshape(2, 128 * m, 64 * m), BF16)


def shards(th, tw, sh, sw):
    x = lax.axis_index("x")
    where = jnp.stack([lax.axis_index(a) for a in ("x", "c", "y", "z")]).astype(jnp.int32)
    piece = sh.shape[0]
    w = sw[:, 0, :]
    place = place_of(ROWS[1])

    def both_ways(r, l):
        return lax.ppermute(r, "x", shift(1)), lax.ppermute(l, "x", shift(-1))

    def others(v, axis):
        return [lax.ppermute(v, axis, shift(k)) for k in (1, 2, 3)]

    def swap(v):
        return lax.ppermute(v, "c", SWAP)

    own, *sends, sh8 = cut(where, th, sh)
    got = [lax.ppermute(s, "x", shift(k + 1)) for k, s in enumerate(sends)]
    other = [swap(v) for v in got]

    every = lax.all_gather(stack(where, piece, sh8, *got), ("y", "z", "c"), axis=0, tiled=True)
    h = gather(where, own, got, other)
    cols = tw.shape[1] // 4

    def product(rows, step):
        block = lax.dynamic_slice(tw, (0, (x + step) % 4 * cols), (tw.shape[0], cols))
        return jnp.dot(rows, block, preferred_element_type=F32)

    n = h.shape[0] // 4
    chains = [both_ways(product(h[i * n : (i + 1) * n], 3), product(h[(i + 2) * n : (i + 3) * n], 1)) for i in (0, 1)]
    p = rest(where, h, tw)
    pick = pick_of(where, piece, (p,))
    before = ()
    for step in (0, 1):
        for i in (0, 1):
            r, l = hop(where, p, step, i, *chains[i], before)
            chains[i] = both_ways(r, l)
            before = (r, pick)
    sl = student(where, pick, every, w, before[:1])
    whole_sums = hop(where, p, 2, 0, *chains[0], (sl,), flops=6 * 10**9)
    tl, st = local(where, p, [*whole_sums, *chains[1]], sl)

    st = merge(where, 1, st, swap(st))
    st = merge(where, 3, st, *others(st, "z"))
    st = merge(where, 2, st, *others(st, "y"))
    grad, away, kl = grad_of(where, [st, *others(st, "x")], tl, sl, place, w)
    got = swap(away)
    chip = add(where, keep_of(where, grad, place, w), got)
    parts = lax.all_to_all(chip.reshape(64, 8, -1), CHIPS, split_axis=0, concat_axis=0, tiled=True)
    grad_weight, done = weight_of(where, every, grad, pick, (chip,))
    mine, theirs = total(where, parts, (done,))
    grad_hidden = join(where, mine, swap(theirs), sh.shape)
    return (kl.reshape(()), grad_hidden, grad_weight)


def solution(mesh):
    mesh = Mesh(mesh.devices.reshape(4, 4, 4, 2), ALL)
    vocab = ("y", "z", "c")
    in_specs = (P("x", None), P("x", vocab), P(ALL, None), P(None, vocab, "x"))
    out_specs = (P(), P(ALL, None), P(None, vocab, "x"))
    return jax.shard_map(shards, mesh=mesh, in_specs=in_specs, out_specs=out_specs, check_vma=False)
```

```python
import functools

import jax
import jax.numpy as jnp
import numpy as np
from jax import lax
from jax.experimental import pallas as pl
from jax.experimental.pallas import tpu as pltpu
from jax.sharding import Mesh
from jax.sharding import PartitionSpec as P

grad_scale = 64.0
ROWS = (8, 4)
ALL = ("x", "y", "z", "c")
CHIPS = ("x", "y", "z")
SWAP = [(0, 1), (1, 0)]
F32, BF16 = jnp.float32, jnp.bfloat16
NT = (((1,), (1,)), ((), ()))
TN = (((0,), (0,)), ((), ()))
MIB = 2**20


def shift(k):
    return [(i, (i + k) % 4) for i in range(4)]


def dot(a, b, dims=(((1,), (0,)), ((), ()))):
    return lax.dot_general(a, b, dims, preferred_element_type=F32)


def call(body, scalars, args, in_specs, outs, out_specs, grid=(1,), flops=0, after=(), spare=4, scratch=()):
    n = 1 + len(args)
    blocks = [(s.block_shape or (), a.dtype) for s, a in zip([*in_specs, *out_specs], [*args, *outs])]
    held = sum(int(np.prod(shape)) * dtype.itemsize for shape, dtype in blocks) * (1 if grid == (1,) else 2)

    def ordered(*refs):
        body(*refs[:n], *refs[n + len(after) :])

    return pl.pallas_call(
        ordered if after else body,
        out_shape=outs,
        grid_spec=pltpu.PrefetchScalarGridSpec(
            num_scalar_prefetch=1,
            grid=grid,
            in_specs=list(in_specs) + [pl.BlockSpec(memory_space=pl.ANY)] * len(after),
            out_specs=out_specs,
            scratch_shapes=scratch,
        ),
        compiler_params=pltpu.CompilerParams(vmem_limit_bytes=held + spare * MIB),
        cost_estimate=pl.CostEstimate(flops=flops, bytes_accessed=0, transcendentals=0),
    )(scalars, *args, *after)


def whole(shape):
    return pl.BlockSpec(shape, lambda *_: (0,) * len(shape))


def sds(shape, dtype):
    return jax.ShapeDtypeStruct(shape, dtype)


def cut_body(where, th, sh, own, s1, s2, s3, sh8):
    ks = th.shape[1] // 4
    x, c = where[0], where[1]
    def block(k):
        return th[:, pl.ds(pl.multiple_of(lax.rem(x + k, 4) * ks, ks), ks)]

    def one_hot(part, of):
        picks = []
        for m, start in zip(ROWS, (0, ROWS[0])):
            n = 16 * m // of
            i = lax.broadcasted_iota(jnp.int32, (n, th.shape[0]), 0) + part * n
            chip = lax.shift_right_logical(i, m.bit_length() - 1)
            row = chip * sum(ROWS) + start + jnp.bitwise_and(i, m - 1)
            picks.append(jnp.where(row == lax.broadcasted_iota(jnp.int32, row.shape, 1), 1.0, 0.0))
        return jnp.concatenate(picks, axis=0).astype(BF16)

    pick = one_hot(c, 2)
    for k, out in ((1, s1), (2, s2), (3, s3)):
        n = pick.shape[0]
        out[:n, :] = dot(pick, block(k)).astype(BF16)
        out[n:, :] = jnp.zeros((16, ks), BF16)
        m, d = sh.shape
        out[n : n + m, :] = sh[:, :ks]
        out[n + 8 : n + 8 + m, : d - ks] = sh[:, ks:]
    own[...] = dot(one_hot(0, 1), block(0)).astype(BF16)
    sh8[...] = jnp.zeros_like(sh8)
    sh8[: sh.shape[0], :] = sh[...]


def cut(where, th, sh):
    rows, d = th.shape
    ks = d // 4
    outs = [sds((rows, ks), BF16)] + [sds((rows // 2 + 16, ks), BF16)] * 3 + [sds((8, sh.shape[1]), BF16)]
    return call(
        cut_body, where, (th, sh), [whole(th.shape), whole(sh.shape)], outs, [whole(o.shape) for o in outs],
        flops=4 * rows * rows * d, spare=8,
    )


def stack_body(piece, where, s0, g1, g2, g3, out, held):
    ks = g1.shape[1]
    held[:8, :] = s0[...]
    for k, ref in enumerate((g1, g2, g3)):
        n = ref.shape[0] - 16
        to = 8 * k + 8
        held[to : to + 8, :ks] = ref[n : n + 8, :]
        held[to : to + 8, ks:] = ref[n + 8 :, : out.shape[1] - ks]
    row = lax.broadcasted_iota(jnp.int32, (out.shape[0], 32), 0)
    source = row
    for k in (1, 2, 3):
        source += jnp.where(row >= k * piece, 8 - piece, 0)
    pick = jnp.where(source == lax.broadcasted_iota(jnp.int32, source.shape, 1), 1.0, 0.0).astype(BF16)
    out[...] = dot(pick, held[...]).astype(BF16)


def stack(where, piece, *pieces):
    d = pieces[0].shape[1]
    out = sds((4 * piece, d), BF16)
    specs = [whole(p.shape) for p in pieces]
    body = functools.partial(stack_body, piece)
    return call(body, where, pieces, specs, [out], [whole(out.shape)], scratch=[pltpu.VMEM((32, d), BF16)])[0]


def pick_body(piece, where, out):
    x = where[0]
    n = 64 * ROWS[0]
    for at, count, m, start in ((0, n, ROWS[0], 0), (n, 64 * ROWS[1], ROWS[1], ROWS[0])):
        i = lax.broadcasted_iota(jnp.int32, (count, 1), 0)
        bits = m.bit_length() - 1
        row = start + jnp.bitwise_and(i, m - 1)
        chip = jnp.bitwise_and(lax.shift_right_logical(i, bits), 15)
        k = jnp.bitwise_and(x + 4 - lax.shift_right_logical(i, bits + 4), 3)
        late = jnp.where(row >= piece, 1, 0)
        source = chip * (8 * piece) + late * (4 * piece) + k * piece + row - piece * late
        col = lax.broadcasted_iota(jnp.int32, (count, out.shape[1]), 1)
        out[at : at + count, :] = jnp.where(col == source, 1.0, 0.0).astype(BF16)


def pick_of(where, piece, after):
    tokens = 64 * sum(ROWS)
    out = sds((tokens, tokens), BF16)
    body = functools.partial(pick_body, piece)
    return call(body, where, (), [], [out], [whole(out.shape)], after=after, spare=8)[0]


def columns(where, tw, step):
    n = tw.shape[1] // 4
    return tw[:, pl.ds(pl.multiple_of(lax.rem(where[0] + step, 4) * n, n), n)]


def gather_body(where, own, g1, g2, g3, o1, o2, o3, h):
    x, c = where[0], where[1]
    for m, start in zip(ROWS, (0, ROWS[0])):
        n = 16 * m
        nh = n // 2
        base, at = 64 * start, 16 * start
        h[pl.ds(pl.multiple_of(base + x * n, nh), n), :] = own[at : at + n, :]
        at = at // 2
        for k, (a, b) in enumerate(((g1, o1), (g2, o2), (g3, o3))):
            to = base + lax.rem(x + 3 - k, 4) * n
            h[pl.ds(pl.multiple_of(to + c * nh, nh), nh), :] = a[at : at + nh, :]
            h[pl.ds(pl.multiple_of(to + (1 - c) * nh, nh), nh), :] = b[at : at + nh, :]


def gather(where, own, got, other):
    out = sds((4 * own.shape[0], own.shape[1]), BF16)
    args = (own, *got, *other)
    return call(gather_body, where, args, [whole(a.shape) for a in args], [out], [whole(out.shape)])[0]


def rest_body(where, h, tw, out):
    half = h.shape[0] // 2
    out[0] = dot(h[...], columns(where, tw, 2))
    out[1, :half, :] = dot(h[:half, :], columns(where, tw, 1))
    out[1, half:, :] = dot(h[half:, :], columns(where, tw, 3))
    out[2] = dot(h[...], columns(where, tw, 0))


def rest(where, h, tw):
    rows, ks = h.shape
    cols = tw.shape[1] // 4
    out = sds((3, rows, cols), F32)
    specs = [whole(h.shape), whole(tw.shape)]
    return call(rest_body, where, (h, tw), specs, [out], [whole(out.shape)], flops=6 * rows * ks * cols, spare=6)[0]


def hop_body(where, pr, pl_, right, left, r, l):
    r[...] = pr[0] + right[...]
    l[...] = pl_[0] + left[...]


def hop(where, p, step, i, right, left, after=(), flops=0):
    n, cols = right.shape
    out = sds(right.shape, F32)
    specs = [pl.BlockSpec((1, n, cols), lambda _, w, j=j: (step, j, 0)) for j in (i, i + 2)]
    specs += [whole(right.shape), whole(left.shape)]
    return call(hop_body, where, (p, p, right, left), specs, [out, out], [whole(out.shape)] * 2, after=after, flops=flops)


def student_body(where, pick, rows, w, sl, total):
    @pl.when(pl.program_id(0) == 0)
    def _():
        total[...] = jnp.zeros_like(total)

    total[...] += dot(rows[...], w[...])

    @pl.when(pl.program_id(0) == pl.num_programs(0) - 1)
    def _():
        rest = total[...]
        out = jnp.zeros_like(rest)
        for _ in range(3):
            part = rest.astype(BF16)
            out += dot(pick[...], part)
            rest -= part.astype(F32)
        sl[...] = out


def student(where, pick, rows, w, after):
    tokens, d = rows.shape
    cols = w.shape[1]
    tile = d // 3
    specs = [
        whole(pick.shape),
        pl.BlockSpec((tokens, tile), lambda i, s: (0, i)),
        pl.BlockSpec((tile, cols), lambda i, s: (i, 0)),
    ]
    out = sds((tokens, cols), F32)
    return call(
        student_body, where, (pick, rows, w), specs, [out], [whole(out.shape)],
        grid=(3,), after=after, spare=38, scratch=[pltpu.VMEM(out.shape, F32)],
    )[0]


def local_body(where, p, r0, l0, r1, l1, sl, tl, st):
    n = r0.shape[0]
    half = 2 * n
    tl[:n, :] = r0[...]
    tl[2 * n : 3 * n, :] = l0[...]
    tl[n : 2 * n, :] = p[0, n : 2 * n, :] + r1[...]
    tl[3 * n :, :] = p[0, 3 * n :, :] + l1[...]
    t, s = tl[...], sl[...]
    t_max = jnp.max(t, axis=1, keepdims=True)
    s_max = jnp.max(s, axis=1, keepdims=True)
    te = jnp.exp(t - t_max)
    t_sum = jnp.sum(te, axis=1, keepdims=True)
    cross = jnp.sum(te * (t - s), axis=1, keepdims=True)
    s_sum = jnp.sum(jnp.exp(s - s_max), axis=1, keepdims=True)
    lane = lax.broadcasted_iota(jnp.int32, (2 * half, 128), 1)
    packed = jnp.zeros((2 * half, 128), F32)
    for i, v in enumerate((t_max, t_sum, cross, s_max, s_sum)):
        packed = jnp.where(lane == i, v, packed)
    st[...] = jnp.transpose(packed)[:8, :]


def local(where, p, chains, sl):
    outs = [sds(sl.shape, F32), sds((8, sl.shape[0]), F32)]
    args = (p, *chains, sl)
    specs = [pl.BlockSpec((1,) + sl.shape, lambda i, s: (2, 0, 0))] + [whole(a.shape) for a in args[1:]]
    return call(local_body, where, args, specs, outs, [whole(o.shape) for o in outs], flops=40 * sl.size, spare=10)


def merged(i, pieces):
    n = len(pieces)
    ordered = []
    for j in range(n):
        v = pieces[0]
        for k in range(1, n):
            v = jnp.where(lax.rem(i - j + n, n) == k, pieces[k], v)
        ordered.append(v)
    t_max = functools.reduce(jnp.maximum, [v[0:1] for v in ordered])
    s_max = functools.reduce(jnp.maximum, [v[3:4] for v in ordered])
    t_w = [jnp.exp(v[0:1] - t_max) for v in ordered]
    s_w = [jnp.exp(v[3:4] - s_max) for v in ordered]
    t_sum = sum(v[1:2] * a for v, a in zip(ordered, t_w))
    cross = sum(v[2:3] * a for v, a in zip(ordered, t_w))
    s_sum = sum(v[4:5] * a for v, a in zip(ordered, s_w))
    return [t_max, t_sum, cross, s_max, s_sum]


def merge_body(axis, where, *refs):
    pieces = [r[...] for r in refs[:-1]]
    rows = merged(where[axis], pieces)
    refs[-1][...] = jnp.concatenate(rows + [jnp.zeros_like(pieces[0][:3])], axis=0)


def merge(where, axis, *pieces):
    shape = pieces[0].shape
    body = functools.partial(merge_body, axis)
    return call(body, where, pieces, [whole(shape)] * len(pieces), [sds(shape, F32)], [whole(shape)])[0]


def back(grad, place, w):
    n = 64 * ROWS[0]
    half = w.shape[0] // 2
    b = grad[n:, :]
    low = dot(dot(place[0], b).astype(BF16), w[:half, :], NT)
    low += dot(dot(place[1], b).astype(BF16), w[half:, :], NT)
    return dot(grad[:n, :], w[...], NT), low


def grad_body(where, own, g1, g2, g3, tl, sl, place, w, g, away, kl):
    t_max, t_sum, cross, s_max, s_sum = merged(where[0], [own[...], g1[...], g2[...], g3[...]])
    rows = cross / t_sum - t_max - jnp.log(t_sum) + s_max + jnp.log(s_sum)
    kl[0, 0] = jnp.sum(rows) / rows.shape[1]
    stats = jnp.concatenate([t_max, grad_scale / t_sum, s_max, grad_scale / s_sum], axis=0)
    stats = jnp.concatenate([stats, jnp.zeros((124, stats.shape[1]), F32)], axis=0)
    cols = jnp.transpose(stats)
    s = jnp.exp(sl[...] - cols[:, 2:3]) * cols[:, 3:4]
    g[...] = (s - jnp.exp(tl[...] - cols[:, 0:1]) * cols[:, 1:2]).astype(BF16)
    split = w.shape[0]
    a, b = back(g[...], place, w)
    away[:, :split] = a.astype(BF16)
    away[:, split:] = b.astype(BF16)


def grad_of(where, pieces, tl, sl, place, w):
    tokens, cols = sl.shape
    d = w.shape[0]
    outs = [sds((tokens, cols), BF16), sds((512, d // 4 * 3), BF16), sds((1, 1), F32)]
    args = (*pieces, tl, sl, place, w)
    specs = [whole(a.shape) for a in args[:-1]] + [pl.BlockSpec((d // 2, cols), lambda i, s: (1 - s[1], 0))]
    out_specs = [whole(o.shape) for o in outs[:2]] + [pl.BlockSpec(memory_space=pltpu.SMEM)]
    return call(grad_body, where, args, specs, outs, out_specs, flops=tokens * cols * d, spare=16)


def keep_body(where, g, place, w, out):
    split = w.shape[0]
    a, b = back(g[...], place, w)
    out[:, :split] = a
    out[:, split:] = b


def keep_of(where, g, place, w):
    tokens, cols = g.shape
    d = w.shape[0]
    out = sds((512, d // 4 * 3), F32)
    specs = [whole(g.shape), whole(place.shape), pl.BlockSpec((d // 2, cols), lambda i, s: (s[1], 0))]
    return call(keep_body, where, (g, place, w), specs, [out], [whole(out.shape)], flops=tokens * cols * d, spare=12)[0]


def add_body(where, kept, got, out):
    out[...] = (kept[...] + got[...].astype(F32)).astype(BF16)


def add(where, kept, got):
    specs = [whole(kept.shape)] * 2
    return call(add_body, where, (kept, got), specs, [sds(kept.shape, BF16)], [whole(kept.shape)], spare=6)[0]


def total_body(where, parts, mine, theirs):
    both = jnp.sum(parts[...].astype(F32), axis=0)
    half = both.shape[1] // 3
    a, b = both[:, : 2 * half], both[:, 2 * half :]
    n = sum(ROWS) // 2
    late = jnp.concatenate([b[: ROWS[1]], b[ROWS[1] :]], axis=1)
    second = jnp.concatenate([a[n:], late, jnp.zeros_like(a[n:])], axis=0)
    mine[...] = jnp.where(where[1] == 0, a, second).astype(BF16)
    theirs[...] = jnp.where(where[1] == 0, second, a).astype(BF16)


def total(where, parts, after):
    out = sds((8, parts.shape[2] // 3 * 2), BF16)
    return call(total_body, where, (parts,), [whole(parts.shape)], [out, out], [whole(out.shape)] * 2, after=after, spare=10)


def join_body(where, mine, got, out):
    half = mine.shape[1]
    n = out.shape[0]
    out[:, pl.ds(pl.multiple_of(where[1] * half, half), half)] = mine[:n, :]
    out[:, pl.ds(pl.multiple_of((1 - where[1]) * half, half), half)] = got[:n, :]


def join(where, mine, got, shape):
    return call(join_body, where, (mine, got), [whole(mine.shape)] * 2, [sds(shape, BF16)], [whole(shape)])[0]


def weight_body(where, rows, g, pick, out, done, placed):
    @pl.when(pl.program_id(0) == 0)
    def _():
        placed[...] = dot(pick[...], g[...], TN).astype(BF16)

    out[...] = dot(rows[...], placed[...], TN)[:, None, :]
    done[...] = jnp.zeros_like(done)


def weight_of(where, rows, g, pick, after):
    tokens, d = rows.shape
    cols = g.shape[1]
    tile = 256
    outs = [sds((d, 1, cols), F32), sds((8, 128), F32)]
    specs = [pl.BlockSpec((tokens, tile), lambda i, s: (0, i)), whole(g.shape), whole(pick.shape)]
    return call(
        weight_body, where, (rows, g, pick), specs, outs,
        [pl.BlockSpec((tile, 1, cols), lambda i, s: (i, 0, 0)), whole((8, 128))],
        grid=(d // tile,), flops=2 * tokens * d * cols, after=after, scratch=[pltpu.VMEM(g.shape, BF16)],
    )


def place_of(m):
    place = np.zeros((2, 64, 2, m, 64, m), np.float32)
    for chip in range(64):
        for r in range(m):
            for h in range(2):
                place[h, chip, h, r, chip, r] = 1.0
    return jnp.asarray(place.reshape(2, 128 * m, 64 * m), BF16)


def shards(th, tw, sh, sw):
    x = lax.axis_index("x")
    where = jnp.stack([lax.axis_index(a) for a in ("x", "c", "y", "z")]).astype(jnp.int32)
    piece = sh.shape[0]
    w = sw[:, 0, :]
    place = place_of(ROWS[1])

    def both_ways(r, l):
        return lax.ppermute(r, "x", shift(1)), lax.ppermute(l, "x", shift(-1))

    def others(v, axis):
        return [lax.ppermute(v, axis, shift(k)) for k in (1, 2, 3)]

    def swap(v):
        return lax.ppermute(v, "c", SWAP)

    own, *sends, sh8 = cut(where, th, sh)
    got = [lax.ppermute(s, "x", shift(k + 1)) for k, s in enumerate(sends)]
    other = [swap(v) for v in got]

    every = lax.all_gather(stack(where, piece, sh8, *got), ("y", "z", "c"), axis=0, tiled=True)
    h = gather(where, own, got, other)
    cols = tw.shape[1] // 4

    def product(rows, step):
        block = lax.dynamic_slice(tw, (0, (x + step) % 4 * cols), (tw.shape[0], cols))
        return jnp.dot(rows, block, preferred_element_type=F32)

    n = h.shape[0] // 4
    chains = [both_ways(product(h[i * n : (i + 1) * n], 3), product(h[(i + 2) * n : (i + 3) * n], 1)) for i in (0, 1)]
    p = rest(where, h, tw)
    pick = pick_of(where, piece, (p,))
    before = ()
    for step in (0, 1):
        for i in (0, 1):
            r, l = hop(where, p, step, i, *chains[i], before)
            chains[i] = both_ways(r, l)
            before = (r, pick)
    sl = student(where, pick, every, w, before[:1])
    whole_sums = hop(where, p, 2, 0, *chains[0], (sl,), flops=6 * 10**9)
    tl, st = local(where, p, [*whole_sums, *chains[1]], sl)

    st = merge(where, 1, st, swap(st))
    st = merge(where, 3, st, *others(st, "z"))
    st = merge(where, 2, st, *others(st, "y"))
    grad, away, kl = grad_of(where, [st, *others(st, "x")], tl, sl, place, w)
    got = swap(away)
    chip = add(where, keep_of(where, grad, place, w), got)
    parts = lax.all_to_all(chip.reshape(64, 8, -1), CHIPS, split_axis=0, concat_axis=0, tiled=True)
    grad_weight, done = weight_of(where, every, grad, pick, (chip,))
    mine, theirs = total(where, parts, (done,))
    grad_hidden = join(where, mine, swap(theirs), sh.shape)
    return (kl.reshape(()), grad_hidden, grad_weight)


def solution(mesh):
    mesh = Mesh(mesh.devices.reshape(4, 4, 4, 2), ALL)
    vocab = ("y", "z", "c")
    in_specs = (P("x", None), P("x", vocab), P(ALL, None), P(None, vocab, "x"))
    out_specs = (P(), P(ALL, None), P(None, vocab, "x"))
    return jax.shard_map(shards, mesh=mesh, in_specs=in_specs, out_specs=out_specs, check_vma=False)
```

```python
import functools

import jax
import jax.numpy as jnp
import numpy as np
from jax import lax
from jax.experimental import pallas as pl
from jax.experimental.pallas import tpu as pltpu
from jax.sharding import Mesh
from jax.sharding import PartitionSpec as P

grad_scale = 64.0
ROWS = (8, 4)
ALL = ("x", "y", "z", "c")
CHIPS = ("x", "y", "z")
SWAP = [(0, 1), (1, 0)]
F32, BF16 = jnp.float32, jnp.bfloat16
NT = (((1,), (1,)), ((), ()))
TN = (((0,), (0,)), ((), ()))
MIB = 2**20


def shift(k):
    return [(i, (i + k) % 4) for i in range(4)]


def dot(a, b, dims=(((1,), (0,)), ((), ()))):
    return lax.dot_general(a, b, dims, preferred_element_type=F32)


def call(body, scalars, args, in_specs, outs, out_specs, grid=(1,), flops=0, after=(), spare=4, scratch=()):
    n = 1 + len(args)
    blocks = [(s.block_shape or (), a.dtype) for s, a in zip([*in_specs, *out_specs], [*args, *outs])]
    held = sum(int(np.prod(shape)) * dtype.itemsize for shape, dtype in blocks) * (1 if grid == (1,) else 2)

    def ordered(*refs):
        body(*refs[:n], *refs[n + len(after) :])

    return pl.pallas_call(
        ordered if after else body,
        out_shape=outs,
        grid_spec=pltpu.PrefetchScalarGridSpec(
            num_scalar_prefetch=1,
            grid=grid,
            in_specs=list(in_specs) + [pl.BlockSpec(memory_space=pl.ANY)] * len(after),
            out_specs=out_specs,
            scratch_shapes=scratch,
        ),
        compiler_params=pltpu.CompilerParams(vmem_limit_bytes=held + spare * MIB),
        cost_estimate=pl.CostEstimate(flops=flops, bytes_accessed=0, transcendentals=0),
    )(scalars, *args, *after)


def whole(shape):
    return pl.BlockSpec(shape, lambda *_: (0,) * len(shape))


def sds(shape, dtype):
    return jax.ShapeDtypeStruct(shape, dtype)


def cut_body(where, th, sh, own, s1, s2, s3, sh8):
    ks = th.shape[1] // 4
    x, c = where[0], where[1]
    def block(k):
        return th[:, pl.ds(pl.multiple_of(lax.rem(x + k, 4) * ks, ks), ks)]

    def one_hot(part, of):
        picks = []
        for m, start in zip(ROWS, (0, ROWS[0])):
            n = 16 * m // of
            i = lax.broadcasted_iota(jnp.int32, (n, th.shape[0]), 0) + part * n
            chip = lax.shift_right_logical(i, m.bit_length() - 1)
            row = chip * sum(ROWS) + start + jnp.bitwise_and(i, m - 1)
            picks.append(jnp.where(row == lax.broadcasted_iota(jnp.int32, row.shape, 1), 1.0, 0.0))
        return jnp.concatenate(picks, axis=0).astype(BF16)

    pick = one_hot(c, 2)
    for k, out in ((1, s1), (2, s2), (3, s3)):
        n = pick.shape[0]
        out[:n, :] = dot(pick, block(k)).astype(BF16)
        out[n:, :] = jnp.zeros((16, ks), BF16)
        m, d = sh.shape
        out[n : n + m, :] = sh[:, :ks]
        out[n + 8 : n + 8 + m, : d - ks] = sh[:, ks:]
    own[...] = dot(one_hot(0, 1), block(0)).astype(BF16)
    sh8[...] = jnp.zeros_like(sh8)
    sh8[: sh.shape[0], :] = sh[...]


def cut(where, th, sh):
    rows, d = th.shape
    ks = d // 4
    outs = [sds((rows, ks), BF16)] + [sds((rows // 2 + 16, ks), BF16)] * 3 + [sds((8, sh.shape[1]), BF16)]
    return call(
        cut_body, where, (th, sh), [whole(th.shape), whole(sh.shape)], outs, [whole(o.shape) for o in outs],
        flops=4 * rows * rows * d, spare=8,
    )


def stack_body(piece, where, s0, g1, g2, g3, out, held):
    ks = g1.shape[1]
    held[:8, :] = s0[...]
    for k, ref in enumerate((g1, g2, g3)):
        n = ref.shape[0] - 16
        to = 8 * k + 8
        held[to : to + 8, :ks] = ref[n : n + 8, :]
        held[to : to + 8, ks:] = ref[n + 8 :, : out.shape[1] - ks]
    row = lax.broadcasted_iota(jnp.int32, (out.shape[0], 32), 0)
    source = row
    for k in (1, 2, 3):
        source += jnp.where(row >= k * piece, 8 - piece, 0)
    pick = jnp.where(source == lax.broadcasted_iota(jnp.int32, source.shape, 1), 1.0, 0.0).astype(BF16)
    out[...] = dot(pick, held[...]).astype(BF16)


def stack(where, piece, *pieces):
    d = pieces[0].shape[1]
    out = sds((4 * piece, d), BF16)
    specs = [whole(p.shape) for p in pieces]
    body = functools.partial(stack_body, piece)
    return call(body, where, pieces, specs, [out], [whole(out.shape)], scratch=[pltpu.VMEM((32, d), BF16)])[0]


def pick_body(piece, where, out):
    x = where[0]
    n = 64 * ROWS[0]
    for at, count, m, start in ((0, n, ROWS[0], 0), (n, 64 * ROWS[1], ROWS[1], ROWS[0])):
        i = lax.broadcasted_iota(jnp.int32, (count, 1), 0)
        bits = m.bit_length() - 1
        row = start + jnp.bitwise_and(i, m - 1)
        chip = jnp.bitwise_and(lax.shift_right_logical(i, bits), 15)
        k = jnp.bitwise_and(x + 4 - lax.shift_right_logical(i, bits + 4), 3)
        late = jnp.where(row >= piece, 1, 0)
        source = chip * (8 * piece) + late * (4 * piece) + k * piece + row - piece * late
        col = lax.broadcasted_iota(jnp.int32, (count, out.shape[1]), 1)
        out[at : at + count, :] = jnp.where(col == source, 1.0, 0.0).astype(BF16)


def pick_of(where, piece, after):
    tokens = 64 * sum(ROWS)
    out = sds((tokens, tokens), BF16)
    body = functools.partial(pick_body, piece)
    return call(body, where, (), [], [out], [whole(out.shape)], after=after, spare=8)[0]


def columns(where, tw, step):
    n = tw.shape[1] // 4
    return tw[:, pl.ds(pl.multiple_of(lax.rem(where[0] + step, 4) * n, n), n)]


def gather_body(where, own, g1, g2, g3, o1, o2, o3, h):
    x, c = where[0], where[1]
    for m, start in zip(ROWS, (0, ROWS[0])):
        n = 16 * m
        nh = n // 2
        base, at = 64 * start, 16 * start
        h[pl.ds(pl.multiple_of(base + x * n, nh), n), :] = own[at : at + n, :]
        at = at // 2
        for k, (a, b) in enumerate(((g1, o1), (g2, o2), (g3, o3))):
            to = base + lax.rem(x + 3 - k, 4) * n
            h[pl.ds(pl.multiple_of(to + c * nh, nh), nh), :] = a[at : at + nh, :]
            h[pl.ds(pl.multiple_of(to + (1 - c) * nh, nh), nh), :] = b[at : at + nh, :]


def gather(where, own, got, other):
    out = sds((4 * own.shape[0], own.shape[1]), BF16)
    args = (own, *got, *other)
    return call(gather_body, where, args, [whole(a.shape) for a in args], [out], [whole(out.shape)])[0]


def rest_body(where, h, tw, out):
    half = h.shape[0] // 2
    out[0] = dot(h[...], columns(where, tw, 2))
    out[1, :half, :] = dot(h[:half, :], columns(where, tw, 1))
    out[1, half:, :] = dot(h[half:, :], columns(where, tw, 3))
    out[2] = dot(h[...], columns(where, tw, 0))


def rest(where, h, tw):
    rows, ks = h.shape
    cols = tw.shape[1] // 4
    out = sds((3, rows, cols), F32)
    specs = [whole(h.shape), whole(tw.shape)]
    return call(rest_body, where, (h, tw), specs, [out], [whole(out.shape)], flops=6 * rows * ks * cols, spare=6)[0]


def hop_body(where, pr, pl_, right, left, r, l):
    r[...] = pr[0] + right[...]
    l[...] = pl_[0] + left[...]


def hop(where, p, step, i, right, left, after=(), flops=0):
    n, cols = right.shape
    out = sds(right.shape, F32)
    specs = [pl.BlockSpec((1, n, cols), lambda _, w, j=j: (step, j, 0)) for j in (i, i + 2)]
    specs += [whole(right.shape), whole(left.shape)]
    return call(hop_body, where, (p, p, right, left), specs, [out, out], [whole(out.shape)] * 2, after=after, flops=flops)


def student_body(where, pick, rows, w, sl, total):
    @pl.when(pl.program_id(0) == 0)
    def _():
        total[...] = jnp.zeros_like(total)

    total[...] += dot(rows[...], w[...])

    @pl.when(pl.program_id(0) == pl.num_programs(0) - 1)
    def _():
        rest = total[...]
        out = jnp.zeros_like(rest)
        for _ in range(3):
            part = rest.astype(BF16)
            out += dot(pick[...], part)
            rest -= part.astype(F32)
        sl[...] = out


def student(where, pick, rows, w, after):
    tokens, d = rows.shape
    cols = w.shape[1]
    tile = d // 3
    specs = [
        whole(pick.shape),
        pl.BlockSpec((tokens, tile), lambda i, s: (0, i)),
        pl.BlockSpec((tile, cols), lambda i, s: (i, 0)),
    ]
    out = sds((tokens, cols), F32)
    return call(
        student_body, where, (pick, rows, w), specs, [out], [whole(out.shape)],
        grid=(3,), after=after, spare=38, scratch=[pltpu.VMEM(out.shape, F32)],
    )[0]


def local_body(where, p, r0, l0, r1, l1, sl, tl, st):
    n = r0.shape[0]
    half = 2 * n
    tl[:n, :] = r0[...]
    tl[2 * n : 3 * n, :] = l0[...]
    tl[n : 2 * n, :] = p[0, n : 2 * n, :] + r1[...]
    tl[3 * n :, :] = p[0, 3 * n :, :] + l1[...]
    t, s = tl[...], sl[...]
    t_max = jnp.max(t, axis=1, keepdims=True)
    s_max = jnp.max(s, axis=1, keepdims=True)
    te = jnp.exp(t - t_max)
    t_sum = jnp.sum(te, axis=1, keepdims=True)
    cross = jnp.sum(te * (t - s), axis=1, keepdims=True)
    s_sum = jnp.sum(jnp.exp(s - s_max), axis=1, keepdims=True)
    lane = lax.broadcasted_iota(jnp.int32, (2 * half, 128), 1)
    packed = jnp.zeros((2 * half, 128), F32)
    for i, v in enumerate((t_max, t_sum, cross, s_max, s_sum)):
        packed = jnp.where(lane == i, v, packed)
    st[...] = jnp.transpose(packed)[:8, :]


def local(where, p, chains, sl):
    outs = [sds(sl.shape, F32), sds((8, sl.shape[0]), F32)]
    args = (p, *chains, sl)
    specs = [pl.BlockSpec((1,) + sl.shape, lambda i, s: (2, 0, 0))] + [whole(a.shape) for a in args[1:]]
    return call(local_body, where, args, specs, outs, [whole(o.shape) for o in outs], flops=40 * sl.size, spare=10)


def merged(i, pieces):
    n = len(pieces)
    ordered = []
    for j in range(n):
        v = pieces[0]
        for k in range(1, n):
            v = jnp.where(lax.rem(i - j + n, n) == k, pieces[k], v)
        ordered.append(v)
    t_max = functools.reduce(jnp.maximum, [v[0:1] for v in ordered])
    s_max = functools.reduce(jnp.maximum, [v[3:4] for v in ordered])
    t_w = [jnp.exp(v[0:1] - t_max) for v in ordered]
    s_w = [jnp.exp(v[3:4] - s_max) for v in ordered]
    t_sum = sum(v[1:2] * a for v, a in zip(ordered, t_w))
    cross = sum(v[2:3] * a for v, a in zip(ordered, t_w))
    s_sum = sum(v[4:5] * a for v, a in zip(ordered, s_w))
    return [t_max, t_sum, cross, s_max, s_sum]


def merge_body(axis, where, *refs):
    pieces = [r[...] for r in refs[:-1]]
    rows = merged(where[axis], pieces)
    refs[-1][...] = jnp.concatenate(rows + [jnp.zeros_like(pieces[0][:3])], axis=0)


def merge(where, axis, *pieces):
    shape = pieces[0].shape
    body = functools.partial(merge_body, axis)
    return call(body, where, pieces, [whole(shape)] * len(pieces), [sds(shape, F32)], [whole(shape)])[0]


def back(grad, place, w):
    n = 64 * ROWS[0]
    half = w.shape[0] // 2
    b = grad[n:, :]
    low = dot(dot(place[0], b).astype(BF16), w[:half, :], NT)
    low += dot(dot(place[1], b).astype(BF16), w[half:, :], NT)
    return dot(grad[:n, :], w[...], NT), low


def grad_body(where, own, g1, g2, g3, tl, sl, place, w, g, away, kl):
    t_max, t_sum, cross, s_max, s_sum = merged(where[0], [own[...], g1[...], g2[...], g3[...]])
    rows = cross / t_sum - t_max - jnp.log(t_sum) + s_max + jnp.log(s_sum)
    kl[0, 0] = jnp.sum(rows) / rows.shape[1]
    stats = jnp.concatenate([t_max, grad_scale / t_sum, s_max, grad_scale / s_sum], axis=0)
    stats = jnp.concatenate([stats, jnp.zeros((124, stats.shape[1]), F32)], axis=0)
    cols = jnp.transpose(stats)
    s = jnp.exp(sl[...] - cols[:, 2:3]) * cols[:, 3:4]
    g[...] = (s - jnp.exp(tl[...] - cols[:, 0:1]) * cols[:, 1:2]).astype(BF16)
    split = w.shape[0]
    a, b = back(g[...], place, w)
    away[:, :split] = a.astype(BF16)
    away[:, split:] = b.astype(BF16)


def grad_of(where, pieces, tl, sl, place, w):
    tokens, cols = sl.shape
    d = w.shape[0]
    outs = [sds((tokens, cols), BF16), sds((512, d // 4 * 3), BF16), sds((1, 1), F32)]
    args = (*pieces, tl, sl, place, w)
    specs = [whole(a.shape) for a in args[:-1]] + [pl.BlockSpec((d // 2, cols), lambda i, s: (1 - s[1], 0))]
    out_specs = [whole(o.shape) for o in outs[:2]] + [pl.BlockSpec(memory_space=pltpu.SMEM)]
    return call(grad_body, where, args, specs, outs, out_specs, flops=tokens * cols * d, spare=16)


def keep_body(where, g, place, w, out):
    split = w.shape[0]
    a, b = back(g[...], place, w)
    out[:, :split] = a
    out[:, split:] = b


def keep_of(where, g, place, w):
    tokens, cols = g.shape
    d = w.shape[0]
    out = sds((512, d // 4 * 3), F32)
    specs = [whole(g.shape), whole(place.shape), pl.BlockSpec((d // 2, cols), lambda i, s: (s[1], 0))]
    return call(keep_body, where, (g, place, w), specs, [out], [whole(out.shape)], flops=tokens * cols * d, spare=12)[0]


def add_body(where, kept, got, out):
    out[...] = (kept[...] + got[...].astype(F32)).astype(BF16)


def add(where, kept, got):
    specs = [whole(kept.shape)] * 2
    return call(add_body, where, (kept, got), specs, [sds(kept.shape, BF16)], [whole(kept.shape)], spare=6)[0]


def total_body(where, parts, mine, theirs):
    both = jnp.sum(parts[...].astype(F32), axis=0)
    half = both.shape[1] // 3
    a, b = both[:, : 2 * half], both[:, 2 * half :]
    n = sum(ROWS) // 2
    late = jnp.concatenate([b[: ROWS[1]], b[ROWS[1] :]], axis=1)
    second = jnp.concatenate([a[n:], late, jnp.zeros_like(a[n:])], axis=0)
    mine[...] = jnp.where(where[1] == 0, a, second).astype(BF16)
    theirs[...] = jnp.where(where[1] == 0, second, a).astype(BF16)


def total(where, parts, after):
    out = sds((8, parts.shape[2] // 3 * 2), BF16)
    return call(total_body, where, (parts,), [whole(parts.shape)], [out, out], [whole(out.shape)] * 2, after=after, spare=10)


def join_body(where, mine, got, out):
    half = mine.shape[1]
    n = out.shape[0]
    out[:, pl.ds(pl.multiple_of(where[1] * half, half), half)] = mine[:n, :]
    out[:, pl.ds(pl.multiple_of((1 - where[1]) * half, half), half)] = got[:n, :]


def join(where, mine, got, shape):
    return call(join_body, where, (mine, got), [whole(mine.shape)] * 2, [sds(shape, BF16)], [whole(shape)])[0]


def weight_body(where, rows, g, pick, out, done, placed):
    @pl.when(pl.program_id(0) == 0)
    def _():
        placed[...] = dot(pick[...], g[...], TN).astype(BF16)

    out[...] = dot(rows[...], placed[...], TN)[:, None, :]
    done[...] = jnp.zeros_like(done)


def weight_of(where, rows, g, pick, after):
    tokens, d = rows.shape
    cols = g.shape[1]
    tile = 256
    outs = [sds((d, 1, cols), F32), sds((8, 128), F32)]
    specs = [pl.BlockSpec((tokens, tile), lambda i, s: (0, i)), whole(g.shape), whole(pick.shape)]
    return call(
        weight_body, where, (rows, g, pick), specs, outs,
        [pl.BlockSpec((tile, 1, cols), lambda i, s: (i, 0, 0)), whole((8, 128))],
        grid=(d // tile,), flops=2 * tokens * d * cols, after=after, scratch=[pltpu.VMEM(g.shape, BF16)],
    )


def place_of(m):
    place = np.zeros((2, 64, 2, m, 64, m), np.float32)
    for chip in range(64):
        for r in range(m):
            for h in range(2):
                place[h, chip, h, r, chip, r] = 1.0
    return jnp.asarray(place.reshape(2, 128 * m, 64 * m), BF16)


def shards(th, tw, sh, sw):
    x = lax.axis_index("x")
    where = jnp.stack([lax.axis_index(a) for a in ("x", "c", "y", "z")]).astype(jnp.int32)
    piece = sh.shape[0]
    w = sw[:, 0, :]
    place = place_of(ROWS[1])

    def both_ways(r, l):
        return lax.ppermute(r, "x", shift(1)), lax.ppermute(l, "x", shift(-1))

    def others(v, axis):
        return [lax.ppermute(v, axis, shift(k)) for k in (1, 2, 3)]

    def swap(v):
        return lax.ppermute(v, "c", SWAP)

    own, *sends, sh8 = cut(where, th, sh)
    got = [lax.ppermute(s, "x", shift(k + 1)) for k, s in enumerate(sends)]
    other = [swap(v) for v in got]

    every = lax.all_gather(stack(where, piece, sh8, *got), ("y", "z", "c"), axis=0, tiled=True)
    h = gather(where, own, got, other)
    cols = tw.shape[1] // 4

    def product(rows, step):
        block = lax.dynamic_slice(tw, (0, (x + step) % 4 * cols), (tw.shape[0], cols))
        return jnp.dot(rows, block, preferred_element_type=F32)

    n = h.shape[0] // 4
    chains, source = [], h
    for i in (0, 1):
        r, l = product(source[i * n : (i + 1) * n], 3), product(source[(i + 2) * n : (i + 3) * n], 1)
        chains.append(both_ways(r, l))
        source = lax.optimization_barrier((h, l))[0]
    p = rest(where, h, tw)
    pick = pick_of(where, piece, (p,))
    before = ()
    for step in (0, 1):
        for i in (0, 1):
            r, l = hop(where, p, step, i, *chains[i], before)
            chains[i] = both_ways(r, l)
            before = (r, pick)
    sl = student(where, pick, every, w, before[:1])
    whole_sums = hop(where, p, 2, 0, *chains[0], (sl,), flops=6 * 10**9)
    tl, st = local(where, p, [*whole_sums, *chains[1]], sl)

    st = merge(where, 1, st, swap(st))
    st = merge(where, 3, st, *others(st, "z"))
    st = merge(where, 2, st, *others(st, "y"))
    grad, away, kl = grad_of(where, [st, *others(st, "x")], tl, sl, place, w)
    got = swap(away)
    chip = add(where, keep_of(where, grad, place, w), got)
    parts = lax.all_to_all(chip.reshape(64, 8, -1), CHIPS, split_axis=0, concat_axis=0, tiled=True)
    grad_weight, done = weight_of(where, every, grad, pick, (chip,))
    mine, theirs = total(where, parts, (done,))
    grad_hidden = join(where, mine, swap(theirs), sh.shape)
    return (kl.reshape(()), grad_hidden, grad_weight)


def solution(mesh):
    mesh = Mesh(mesh.devices.reshape(4, 4, 4, 2), ALL)
    vocab = ("y", "z", "c")
    in_specs = (P("x", None), P("x", vocab), P(ALL, None), P(None, vocab, "x"))
    out_specs = (P(), P(ALL, None), P(None, vocab, "x"))
    return jax.shard_map(shards, mesh=mesh, in_specs=in_specs, out_specs=out_specs, check_vma=False)
```
